512 devices in a mesh: dp: 16 (over y, z_hi), row: 8 (over x, core), col: 4 (over z_lo).
Axes of the slice: x: 4, y: 4, z: 16 (z_hi: 4, z_lo: 4; z = z_hi * 4 + z_lo), core: 2. Of those that a mesh axis runs over, the one named last changes fastest.
Arguments:
- features: bfloat16 [16, 160, 160, 640], P('dp', 'row', 'col'), may hold values from -800 to 800
- hole_mask: int32 [16, 160, 160], P('dp', 'row', 'col'), may hold values 0 or 1
- norm_gain: float32 [640], replicated, may hold values from 0.5 to 1.5
- norm_shift: float32 [640], replicated, may hold values from -3 to 3
- conv_weight: bfloat16 [9, 640, 640], P(None, 'dp'), may hold values from -0.078125 to 0.078125
- mask_weight: float32 [9, 640], replicated, may hold values from -3 to 3
- conv_bias: float32 [640], replicated, may hold values from -3 to 3
Outputs:
- conv_out: bfloat16 [16, 160, 160, 640], P('dp', 'row', 'col')
The draws below stay inside these ranges and needn't reach their ends.
All inputs are finite; a program needn't handle non-finite values. No bound on the sum of `hole_mask` on one device may be relied on, other than what follows from the above.
Results may differ from the reference program's by a relative error of at most 0.0032.
Values may be sent and summed in bfloat16 or wider, within the bound.
A program may use at most 128 MiB of HBM per device.

```python
import jax
import jax.numpy as jnp
from jax import lax

CH = 640
GROUPS = 32
ROWS_DEV = 20
COLS_DEV = 40
IMG_H = 160
IMG_W = 160
BATCH = 16


def draw_features(key, part):
    key_base, key_chan, key_offset, key_tile = jax.random.split(key, 4)
    shape = (BATCH, IMG_H, IMG_W, CH)
    rows = jnp.arange(IMG_H, dtype=jnp.float32) / max(IMG_H - 1, 1)
    cols = jnp.arange(IMG_W, dtype=jnp.float32) / max(IMG_W - 1, 1)
    ramp = jnp.power(3.0, rows - 0.5)[:, None] * jnp.power(3.0, cols - 0.5)[None, :]
    tile_rows = max(ROWS_DEV // 2, 1)
    tile_cols = max(COLS_DEV // 4, 1)
    row_tiles = (IMG_H + tile_rows - 1) // tile_rows
    col_tiles = (IMG_W + tile_cols - 1) // tile_cols
    tile_power = jax.random.uniform(key_tile, (BATCH, row_tiles, col_tiles), jnp.float32, -1.0, 1.0)
    tile_gain = jnp.power(3.0, tile_power)
    row_index = jnp.arange(IMG_H) // tile_rows
    col_index = jnp.arange(IMG_W) // tile_cols
    spatial = tile_gain[:, row_index[:, None], col_index[None, :]] * ramp[None, :, :]
    base = jax.random.truncated_normal(key_base, -4.0, 4.0, shape, jnp.float32)
    offset = jax.random.uniform(key_offset, (BATCH, 1, 1, CH), jnp.float32, -1.0, 1.0)
    chan = jnp.power(10.0, jax.random.uniform(key_chan, (CH,), jnp.float32, 0.0, 1.0))
    return ((base + offset) * spatial[:, :, :, None] * chan).astype(jnp.bfloat16)


def with_ends(values, own_key, least, largest):
    longest = values.shape.index(max(values.shape))
    spots = []
    for shift in (0, 1):
        where = [jax.random.randint(jax.random.fold_in(own_key, axis), (), 0, length) for axis, length in enumerate(values.shape)]
        where[longest] = (where[longest] + shift) % values.shape[longest]
        spots.append(tuple(where))
    return values.at[spots[0]].set(least).at[spots[1]].set(largest)


def levels(key, dims, pieces, low, top_value):
    factor_of, own = 1.0, jax.random.fold_in(key, 6)
    for dim, shards_of in pieces:
        heights = jnp.exp(jax.random.uniform(jax.random.fold_in(own, dim), (shards_of,), jnp.float32, low / len(pieces), top_value / len(pieces)))
        factor_of = factor_of * jnp.repeat(heights, dims[dim] // shards_of).reshape([-1 if axis == dim else 1 for axis in range(len(dims))])
    return factor_of


def scatter_about(own_key, dims, width, bound, cuts=(), kind=jnp.bfloat16):
    loudness = levels(own_key, dims, cuts, -0.22, 0.18) if cuts else 1.0
    drawn = jax.random.normal(own_key, dims, jnp.float32) * width * loudness
    return jnp.minimum(jnp.maximum(drawn, -bound), bound).astype(kind)


def setup_inputs(seed: int = 0) -> dict:
    key_list = jax.random.split(jax.random.key(seed), 8)
    return {
        "features": draw_features(jax.random.fold_in(key_list[7], 71), 0),
        "hole_mask": with_ends((jax.random.randint(key_list[1], (BATCH, IMG_H, IMG_W), 0, 2) < 1).astype(jnp.int32), jax.random.fold_in(key_list[1], 1), 0, 1),
        "norm_gain": jnp.clip(jax.random.uniform(key_list[2], (CH,), jnp.float32, 0.5, 1.5), 0.5, 1.5),
        "norm_shift": scatter_about(key_list[3], (CH,), 0.5, 3.0, (), jnp.float32),
        "conv_weight": scatter_about(key_list[4], (9, CH, CH), (9 * CH) ** -0.5, 0.078125, ((1, 16),)),
        "mask_weight": scatter_about(key_list[5], (9, CH), 0.5, 3.0, (), jnp.float32),
        "conv_bias": scatter_about(key_list[6], (CH,), 0.5, 3.0, (), jnp.float32),
    }


EPS = 1e-05

def reference(features, hole_mask, norm_gain, norm_shift, conv_weight, mask_weight, conv_bias):
    weight_full = conv_weight.astype(jnp.float32)

    def one_image(pair):
        image, holes = pair
        grouped = image.astype(jnp.float32).reshape(IMG_H, IMG_W, GROUPS, CH // GROUPS)
        mean_val = lax.optimization_barrier(jnp.mean(grouped, axis=(0, 1, 3)))
        deviate = grouped - mean_val[None, None, :, None]
        var_val = lax.optimization_barrier(jnp.mean(deviate * deviate, axis=(0, 1, 3)))
        normed = (deviate * lax.rsqrt(var_val + EPS)[None, None, :, None]).reshape(IMG_H, IMG_W, CH)
        act_low = jax.nn.silu(normed * norm_gain + norm_shift).astype(jnp.bfloat16)
        act_full = lax.optimization_barrier(act_low).astype(jnp.float32)
        padded = jnp.pad(act_full, ((1, 1), (1, 1), (0, 0)))
        mask_pad = jnp.pad(holes.astype(jnp.float32), 1)
        total = jnp.zeros((IMG_H, IMG_W, CH), jnp.float32) + conv_bias
        for tap in range(9):
            row_off = tap // 3
            col_off = tap % 3
            window = padded[row_off:row_off + IMG_H, col_off:col_off + IMG_W].reshape(IMG_H * IMG_W, CH)
            prod = jnp.dot(window, weight_full[tap], precision=lax.Precision.HIGHEST, preferred_element_type=jnp.float32)
            total = total + prod.reshape(IMG_H, IMG_W, CH)
            total = total + mask_pad[row_off:row_off + IMG_H, col_off:col_off + IMG_W, None] * mask_weight[tap]
        return total.astype(jnp.bfloat16)
    return lax.map(one_image, (features, hole_mask))
```

```python
import jax
import jax.numpy as jnp
from jax import lax
from jax.experimental import pallas as pl
from jax.experimental.pallas import tpu as pltpu
from jax.sharding import PartitionSpec as P

GROUPS = 32
EPS = 1e-05
MESH = pl.DeviceIdType.MESH
BF = jnp.bfloat16
F32 = jnp.float32
R, C, CH = 20, 40, 640
BLK = 240
CUT = 128
STRIDE = 56
DELTAS = (0, 3, 1, 2)


def dot(a, b):
    return jnp.dot(a, b, preferred_element_type=F32)


def dot3(a, b):
    hi = a.astype(BF)
    rest = a - hi.astype(F32)
    mid = rest.astype(BF)
    low = (rest - mid.astype(F32)).astype(BF)
    return dot(hi, b) + dot(mid, b) + dot(low, b)


def kernel(
    feat, mask, gain, shift, weight, mask_w, bias, out,
    wall, wm, act, even, odd, acc, col_out, row_in, col_in, cor_in,
    mask_in, mpad, mcols, mtaps, gtab, st_out, st_in,
    z_s, z_r, f_s, f_r, fh_s, fh_r, l_s, l_r, lh_s, lh_r, c_s, c_r, h_s, h_r, t_s, t_r,
):
    dp, row, col = lax.axis_index("dp"), lax.axis_index("row"), lax.axis_index("col")
    x, core = row // 2, row % 2
    y, zh = dp // 4, dp % 4

    def at(y_, zh_, x_, core_, col_):
        return (y_ * 4 + zh_, x_ * 2 + core_, col_)

    up, down = (row + 7) % 8, (row + 1) % 8
    left, right = (col + 3) % 4, (col + 1) % 4
    group = [(dp, (row + i) % 8, (col + j) % 4) for i in range(8) for j in range(4) if i or j]
    far = [at(y, (zh + s) % 4, x, core, col) for s in (1, 3, 2)]
    xn = [at(y, zh, (x + 1) % 4, core, col), at(y, zh, (x + 3) % 4, core, col)]
    yn = [at((y + 1) % 4, zh, x, core, col), at((y + 3) % 4, zh, x, core, col)]
    first = core == 0
    fdev = [tuple(jnp.where(first, a, b) for a, b in zip(yn[i], xn[i])) for i in range(2)]
    ldev = [tuple(jnp.where(first, b, a) for a, b in zip(yn[i], xn[i])) for i in range(2)]
    sib = at(y, zh, x, 1 - core, col)
    fme = jnp.where(first, y, x)
    lme = jnp.where(first, x, y)
    zof = [(zh + d) % 4 for d in DELTAS]

    barrier = pltpu.get_barrier_semaphore()
    peers = far + yn + group
    for d in peers:
        pl.semaphore_signal(barrier, inc=1, device_id=d, device_id_type=MESH)

    isodd = zh % 2 == 1
    zero8 = jnp.zeros((8, CH), F32)

    def both(a, b):
        return jnp.where(isodd, b, a)

    def pair(j):
        s, t = weight[2 * j].astype(F32), weight[2 * j + 1].astype(F32)
        a = jnp.concatenate([s, t[32:40], t[0:32]], axis=0)
        b = jnp.concatenate([s[8:40], t[0:8], s[0:8], t[8:40]], axis=0)
        return both(a, b).astype(BF)

    @pl.when(first)
    def _():
        v = pair(x)
        for n in range(3):
            wall[0, zh, x, y, 80 * n : 80 * n + 80, :] = v[:, 128 * n : 128 * n + 128]

    @pl.when(jnp.logical_not(first))
    def _():
        last = weight[8].astype(F32)
        tail = both(
            jnp.concatenate([last, zero8], axis=0), jnp.concatenate([zero8, last], axis=0)
        ).astype(BF)
        for j in range(4):
            v = pair(j)
            for n in range(2):
                wall[1, zh, y, j, 80 * n : 80 * n + 80, :] = v[:, 384 + 128 * n : 512 + 128 * n]
            for s in range(4):
                m = 4 * j + s
                if m < 15:
                    n, r = m // 3, m % 3
                    wall[1, zh, y, j, 160 + 16 * s : 176 + 16 * s, :] = tail[
                        16 * r : 16 * r + 16, 128 * n : 128 * n + 128
                    ]
                else:
                    wall[1, zh, y, j, 160 + 16 * s : 176 + 16 * s, :] = jnp.zeros((16, 128), BF)
            wall[1, zh, y, j, 224:240, :] = jnp.zeros((16, 128), BF)

    def pass1(r, total):
        v = feat[r].astype(F32)
        col_out[0, pl.ds(r, 1), :] = v[0:1]
        col_out[1, pl.ds(r, 1), :] = v[39:40]
        return total + v[0:8] + v[8:16] + v[16:24] + v[24:32] + v[32:40]

    zeros = jnp.zeros((8, CH), F32)
    col_out[0, 16:24, :] = zeros
    col_out[1, 16:24, :] = zeros
    total = lax.fori_loop(0, R, pass1, zeros)

    pl.semaphore_wait(barrier, len(peers))

    def copy(src, dst, s, r, d):
        return pltpu.make_async_remote_copy(src, dst, s, r, device_id=d, device_id_type=MESH)

    def zc(i):
        blk = wall.at[core, zh, lme, fme]
        return copy(blk, blk, z_s.at[i], z_r.at[i], far[i])

    def zin(k):
        i = {3: 0, 1: 1, 2: 2}[DELTAS[k]]
        blk = wall.at[core, zof[k], lme, fme]
        return copy(blk, blk, z_s.at[i], z_r.at[i], far[i])

    def fc(k, i, who):
        blk = wall.at[core, zof[k], lme, (fme + who) % 4]
        return copy(blk, blk, f_s.at[k, i], f_r.at[k, i], fdev[i])

    def fhc(k, i, who):
        rows = pl.ds(0, CUT) if i == 0 else pl.ds(CUT, BLK - CUT)
        blk = wall.at[core, zof[k], lme, (fme + who) % 4, rows]
        return copy(blk, blk, fh_s.at[k, i], fh_r.at[k, i], fdev[i])

    def lc(k, i, who):
        blk = wall.at[core, zof[k], (lme + who) % 4]
        return copy(blk, blk, l_s.at[k, i], l_r.at[k, i], ldev[i])

    def lhc(k, i, who):
        blk = wall.at[core, zof[k], (lme + who) % 4, pl.ds(2 * i, 2)]
        return copy(blk, blk, lh_s.at[k, i], lh_r.at[k, i], ldev[i])

    def sc(k, which):
        blk = wall.at[which, zof[k]]
        return copy(blk, blk, c_s.at[k], c_r.at[k], sib)

    def f_send(k):
        fc(k, 0, 0).start()
        fc(k, 1, 0).start()

    def f_fwd(k):
        fc(k, 0, 3).wait_recv()
        fhc(k, 0, 3).start()
        fc(k, 1, 1).wait_recv()
        fhc(k, 1, 1).start()

    def f_done(k):
        fhc(k, 0, 2).wait_recv()
        fhc(k, 1, 2).wait_recv()

    def f_sent(k):
        fc(k, 0, 0).wait_send()
        fc(k, 1, 0).wait_send()
        fhc(k, 0, 3).wait_send()
        fhc(k, 1, 1).wait_send()

    def l_send(k):
        lc(k, 0, 0).start()
        lc(k, 1, 0).start()

    def l_fwd(k):
        lc(k, 0, 3).wait_recv()
        lhc(k, 0, 3).start()
        lc(k, 1, 1).wait_recv()
        lhc(k, 1, 1).start()

    def l_done(k):
        lhc(k, 0, 2).wait_recv()
        lhc(k, 1, 2).wait_recv()

    def l_sent(k):
        lc(k, 0, 0).wait_send()
        lc(k, 1, 0).wait_send()
        lhc(k, 0, 3).wait_send()
        lhc(k, 1, 1).wait_send()

    for i in range(3):
        zc(i).start()

    @pl.when(first)
    def _():
        f_send(0)

    @pl.when(jnp.logical_not(first))
    def _():
        l_send(0)

    halo = [
        (feat.at[R - 1], row_in.at[0], (dp, down, col)),
        (feat.at[0], row_in.at[1], (dp, up, col)),
        (col_out.at[1], col_in.at[0], (dp, row, right)),
        (col_out.at[0], col_in.at[1], (dp, row, left)),
        (col_out.at[1, pl.ds(16, 8)], cor_in.at[0], (dp, down, right)),
        (col_out.at[0, pl.ds(16, 8)], cor_in.at[1], (dp, down, left)),
        (col_out.at[1, pl.ds(0, 8)], cor_in.at[2], (dp, up, right)),
        (col_out.at[0, pl.ds(0, 8)], cor_in.at[3], (dp, up, left)),
    ]
    around = [
        (dp, down, right), (dp, down, col), (dp, down, left),
        (dp, row, right), (dp, row, left),
        (dp, up, right), (dp, up, col), (dp, up, left),
    ]
    halo += [(mask, mask_in.at[i], d) for i, d in enumerate(around)]
    hcs = [copy(s, d, h_s.at[i], h_r.at[i], dev) for i, (s, d, dev) in enumerate(halo)]
    for c in hcs:
        c.start()

    chan = lax.broadcasted_iota(jnp.int32, (CH, 128), 0)
    lane = lax.broadcasted_iota(jnp.int32, (CH, 128), 1)
    per = CH // GROUPS
    gm = jnp.where((chan >= lane * per) & (chan < lane * per + per), 1.0, 0.0).astype(BF)
    lane_t = lax.broadcasted_iota(jnp.int32, (128, CH), 0)
    chan_t = lax.broadcasted_iota(jnp.int32, (128, CH), 1)
    gt = jnp.where((chan_t >= lane_t * per) & (chan_t < lane_t * per + per), 1.0, 0.0).astype(BF)

    def spread(v):
        return jnp.broadcast_to(jnp.sum(v, axis=0, keepdims=True), v.shape)

    n_here = float(R * C * per)
    mean_here = dot3(spread(total), gm) * (1.0 / n_here)
    mean_chan = dot3(mean_here, gt)[0:1]

    def pass2(r, total):
        d = feat[r].astype(F32) - mean_chan
        d = d * d
        return total + d[0:8] + d[8:16] + d[16:24] + d[24:32] + d[32:40]

    m2 = dot3(spread(lax.fori_loop(0, R, pass2, zeros)), gm)
    sub = lax.broadcasted_iota(jnp.int32, (8, 128), 0)
    st_out[...] = jnp.where(sub == 0, mean_here, m2)
    tcs = [copy(st_out, st_in.at[i], t_s.at[i], t_r.at[i], d) for i, d in enumerate(group)]
    for c in tcs:
        c.start()

    @pl.when(first)
    def _():
        f_fwd(0)
        f_done(0)
        l_send(0)

    zin(1).wait_recv()
    f_send(1)
    zin(2).wait_recv()
    f_send(2)

    for c in hcs[8:]:
        c.wait_recv()

    lane1 = lax.broadcasted_iota(jnp.int32, (R, 128), 1)

    def wide(v):
        return jnp.concatenate([v.astype(F32), jnp.zeros((R, 128 - C), F32)], axis=1)

    def strip(lef, mid, rig):
        a = pltpu.roll(wide(lef), 128 - 39, 1)
        b = pltpu.roll(wide(mid), 1, 1)
        c = pltpu.roll(wide(rig), 41, 1)
        res = jnp.where((lane1 >= 1) & (lane1 <= 40), b, 0.0)
        res = jnp.where((lane1 == 0) & (col > 0), a, res)
        return jnp.where((lane1 == 41) & (col < 3), c, res)

    above = strip(mask_in[0], mask_in[1], mask_in[2])
    here = strip(mask_in[3], mask[...], mask_in[4])
    below = strip(mask_in[5], mask_in[6], mask_in[7])
    mpad[...] = jnp.zeros((128, 128), F32)
    mpad[0:1, :] = jnp.where(row > 0, above[19:20], 0.0)
    mpad[1:21, :] = here
    mpad[21:22, :] = jnp.where(row < 7, below[0:1], 0.0)
    mcols[...] = mpad[...].T
    d3 = mcols[0:40, :] + pltpu.roll(mcols[1:41, :], 32, 1) + pltpu.roll(mcols[2:42, :], 64, 1)

    def fill_mask(p, _):
        a = pltpu.roll(d3, lax.rem(128 - 2 * p, 128), 1)
        b = pltpu.roll(d3, lax.rem(127 - 2 * p, 128), 1)
        mtaps[pl.ds(pl.multiple_of(80 * p, 80), 80), :] = jnp.concatenate([a, b], axis=0).astype(BF)
        return 0

    lax.fori_loop(0, 10, fill_mask, 0)
    gtab[...] = jnp.zeros((128, CH), F32)
    for dy in range(3):
        for dx in range(3):
            gtab[32 * dx + dy : 32 * dx + dy + 1, :] = mask_w[3 * dy + dx : 3 * dy + dx + 1, :]
    g = gtab[...]
    g_hi = g.astype(BF)
    g_rest = g - g_hi.astype(F32)
    g_mid = g_rest.astype(BF)
    g_low = (g_rest - g_mid.astype(F32)).astype(BF)
    bias_row = bias[...]

    def mask_term(p, _):
        rows = pl.ds(pl.multiple_of(80 * p, 80), 80)
        m = mtaps[rows, :]
        acc[rows, :] = dot(m, g_hi) + dot(m, g_mid) + dot(m, g_low) + bias_row
        return 0

    lax.fori_loop(0, 10, mask_term, 0)

    f_fwd(1)
    f_fwd(2)

    for c in tcs:
        c.wait_recv()
    means = st_out[0:1, :]
    for i in range(31):
        means = means + st_in[i, 0:1, :]
    mean_g = means * (1.0 / 32.0)
    dm = st_out[0:1, :] - mean_g
    sq = st_out[1:2, :] + n_here * dm * dm
    for i in range(31):
        dm = st_in[i, 0:1, :] - mean_g
        sq = sq + st_in[i, 1:2, :] + n_here * dm * dm
    rs_g = lax.rsqrt(sq * (1.0 / (32.0 * n_here)) + EPS)
    both_g = dot3(jnp.concatenate([mean_g, rs_g, jnp.zeros((6, 128), F32)], axis=0), gt)
    mean_c, rs_c = both_g[0:1], both_g[1:2]
    gain_c, shift_c = gain[...], shift[...]

    def activate(v):
        v = (v - mean_c) * rs_c * gain_c + shift_c
        return v / (1.0 + jnp.exp(-v))

    f_done(1)
    l_send(1)
    f_done(2)
    l_send(2)

    def act_row(r, _):
        act[r + 1, 8 : 8 + C, :] = activate(feat[r].astype(F32))
        return 0

    lax.fori_loop(0, R, act_row, 0)
    for c in hcs[:8]:
        c.wait_recv()
    act[0, 8 : 8 + C, :] = jnp.where(row > 0, activate(row_in[0].astype(F32)), 0.0)
    act[21, 8 : 8 + C, :] = jnp.where(
        row < 7, activate(row_in[1].astype(F32)), 0.0
    )
    for side, there, off in ((0, col > 0, 7), (1, col < 3, 48)):
        edge = jnp.where(there, activate(col_in[side]), 0.0)
        for r in range(R):
            act[r + 1, off : off + 1, :] = edge[r : r + 1]
    for i, (there, pick, r, spot) in enumerate((
        ((row > 0) & (col > 0), 3, 0, 7),
        ((row > 0) & (col < 3), 3, 0, 48),
        ((row < 7) & (col > 0), 0, 21, 7),
        ((row < 7) & (col < 3), 0, 21, 48),
    )):
        corner = jnp.where(there, activate(cor_in[i]), 0.0)
        act[r, spot : spot + 1, :] = corner[pick : pick + 1]

    l_fwd(0)
    zin(3).wait_recv()
    f_send(3)

    def taps(p, first_row):
        r = 2 * p + first_row
        res = []
        for dx in range(3):
            a = act[r, 7 + dx : 7 + dx + C, :]
            b = act[r + 1, 7 + dx : 7 + dx + C, :]
            res.append(jnp.concatenate([a, b], axis=0).astype(BF))
        return res

    def fill_even(p, _):
        for dx, v in enumerate(taps(p, 0)):
            even[dx, pl.ds(pl.multiple_of(80 * p, 80), 80), :] = v
        return 0

    def fill_odd(p, _):
        for dx, v in enumerate(taps(p, 1)):
            odd[dx, pl.ds(pl.multiple_of(80 * p, 80), 80), :] = v
        return 0

    lax.fori_loop(0, 11, fill_even, 0)
    l_done(0)
    sc(0, core).start()
    l_fwd(1)
    f_fwd(3)
    lax.fori_loop(0, 10, fill_odd, 0)
    l_fwd(2)
    f_done(3)
    l_send(3)
    l_done(1)
    sc(1, core).start()
    l_done(2)
    sc(2, core).start()
    l_fwd(3)
    l_done(3)
    sc(3, core).start()
    for k in range(4):
        sc(k, 1 - core).wait_recv()

    low_half = lax.broadcasted_iota(jnp.int32, (16, 128), 0) < 8

    def merge(i, _):
        yy, zz = i // 2, 2 * (i % 2)
        base = pl.multiple_of((4 * yy + zz) * 40, 80)
        for j in range(4):
            for n in range(5):
                if n < 3:
                    a = wall.at[0, zz, j, yy, pl.ds(80 * n, 80)]
                    b = wall.at[0, zz + 1, j, yy, pl.ds(80 * n, 80)]
                else:
                    a = wall.at[1, zz, yy, j, pl.ds(80 * (n - 3), 80)]
                    b = wall.at[1, zz + 1, yy, j, pl.ds(80 * (n - 3), 80)]
                a2, b2 = a[32:48, :].astype(F32), b[32:48, :].astype(F32)
                mid_s = jnp.where(low_half, a2, b2).astype(BF)
                mid_t = jnp.concatenate([a2[8:16], b2[0:8]], axis=0).astype(BF)
                ln = pl.ds(128 * n, 128)
                wm[2 * j, pl.ds(base, 80), ln] = jnp.concatenate(
                    [a[0:32, :], mid_s, b[0:32, :]], axis=0
                )
                wm[2 * j + 1, pl.ds(base, 80), ln] = jnp.concatenate(
                    [a[48:80, :], mid_t, b[48:80, :]], axis=0
                )
        for n in range(5):
            def tile(z_, r):
                m = 3 * n + r
                return wall[1, z_, yy, m // 4, pl.ds(160 + 16 * (m % 4), 16), :]
            mid = jnp.where(low_half, tile(zz, 2).astype(F32), tile(zz + 1, 0).astype(F32))
            wm[8, pl.ds(base, 80), pl.ds(128 * n, 128)] = jnp.concatenate(
                [tile(zz, 0), tile(zz, 1), mid.astype(BF), tile(zz + 1, 1), tile(zz + 1, 2)], axis=0
            )
        return 0

    lax.fori_loop(0, 8, merge, 0)

    for dy in range(3):
        def conv(dx, _):
            lhs = odd[dx] if dy == 1 else even[dx, pl.ds(40 * dy, 800), :]
            acc[...] += dot(lhs, wm[3 * dy + dx])
            return 0

        lax.fori_loop(0, 3, conv, 0)
    out[...] = acc[...].astype(BF)

    for i in range(3):
        zc(i).wait_send()

    @pl.when(first)
    def _():
        f_sent(0)

    for k in range(1, 4):
        f_sent(k)
    for k in range(4):
        l_sent(k)
        sc(k, core).wait_send()
    for c in hcs + tcs:
        c.wait_send()


def local(features, hole_mask, norm_gain, norm_shift, conv_weight, mask_weight, conv_bias):
    vm = pl.BlockSpec(memory_space=pltpu.VMEM)
    dma = pltpu.SemaphoreType.DMA
    result = pl.pallas_call(
        kernel,
        out_shape=jax.ShapeDtypeStruct((R * C, CH), BF),
        in_specs=[vm] * 7,
        out_specs=vm,
        scratch_shapes=[
            pltpu.VMEM((2, 4, 4, 4, BLK, 128), BF),
            pltpu.VMEM((9, CH, CH), BF),
            pltpu.VMEM((22, STRIDE, CH), F32),
            pltpu.VMEM((3, 22 * C, CH), BF),
            pltpu.VMEM((3, R * C, CH), BF),
            pltpu.VMEM((R * C, CH), F32),
            pltpu.VMEM((2, 24, CH), F32),
            pltpu.VMEM((2, C, CH), BF),
            pltpu.VMEM((2, 24, CH), F32),
            pltpu.VMEM((4, 8, CH), F32),
            pltpu.VMEM((8, R, C), jnp.int32),
            pltpu.VMEM((128, 128), F32),
            pltpu.VMEM((128, 128), F32),
            pltpu.VMEM((R * C, 128), BF),
            pltpu.VMEM((128, CH), F32),
            pltpu.VMEM((8, 128), F32),
            pltpu.VMEM((31, 8, 128), F32),
            dma((3,)), dma((3,)),
            dma((4, 2)), dma((4, 2)), dma((4, 2)), dma((4, 2)),
            dma((4, 2)), dma((4, 2)), dma((4, 2)), dma((4, 2)),
            dma((4,)), dma((4,)), dma((16,)), dma((16,)), dma((31,)), dma((31,)),
        ],
        compiler_params=pltpu.CompilerParams(
            collective_id=0, has_side_effects=True, vmem_limit_bytes=56 << 20
        ),
        name="conv",
    )(
        features[0], hole_mask[0], norm_gain.reshape(1, CH), norm_shift.reshape(1, CH),
        conv_weight, mask_weight, conv_bias.reshape(1, CH),
    )
    return result.reshape(1, R, C, CH)


def solution(mesh):
    image = P("dp", "row", "col", None)
    return jax.shard_map(
        local,
        mesh=mesh,
        in_specs=(image, P("dp", "row", "col"), P(), P(), P(None, "dp", None), P(), P()),
        out_specs=image,
        check_vma=False,
    )
```

```python
import jax
import jax.numpy as jnp
from jax import lax
from jax.experimental import pallas as pl
from jax.experimental.pallas import tpu as pltpu
from jax.sharding import PartitionSpec as P

GROUPS = 32
EPS = 1e-05
MESH = pl.DeviceIdType.MESH
BF = jnp.bfloat16
F32 = jnp.float32
R, C, CH = 20, 40, 640
BLK = 240
CUT = 128
STRIDE = 56
DELTAS = (0, 3, 1, 2)


def dot(a, b):
    return jnp.dot(a, b, preferred_element_type=F32)


def dot3(a, b):
    hi = a.astype(BF)
    rest = a - hi.astype(F32)
    mid = rest.astype(BF)
    low = (rest - mid.astype(F32)).astype(BF)
    return dot(hi, b) + dot(mid, b) + dot(low, b)


def kernel(
    feat4, mask3, gain, shift, weight, mask_w, bias, out4,
    wall, wm, act, taps, acc, feat, col_out, row_in, col_in, cor_in,
    mask_in, mpad, mcols, mtaps, gtab, st_out, st_in,
    z_s, z_r, f_s, f_r, fh_s, fh_r, p_s, p_r, q_s, q_r, c_s, c_r, h_s, h_r, t_s, t_r, in_sem, feat_raw,
):
    mask = mask3.at[0]
    dp, row, col = lax.axis_index("dp"), lax.axis_index("row"), lax.axis_index("col")
    x, core = row // 2, row % 2
    y, zh = dp // 4, dp % 4

    def at(y_, zh_, x_, core_, col_):
        return (y_ * 4 + zh_, x_ * 2 + core_, col_)

    up, down = (row + 7) % 8, (row + 1) % 8
    left, right = (col + 3) % 4, (col + 1) % 4
    far = [at(y, (zh + s) % 4, x, core, col) for s in (1, 3, 2)]
    xn = [at(y, zh, (x + 1) % 4, core, col), at(y, zh, (x + 3) % 4, core, col)]
    yn = [at((y + 1) % 4, zh, x, core, col), at((y + 3) % 4, zh, x, core, col)]
    first = core == 0
    fdev = [tuple(jnp.where(first, a, b) for a, b in zip(yn[i], xn[i])) for i in range(2)]
    ldev = [tuple(jnp.where(first, b, a) for a, b in zip(yn[i], xn[i])) for i in range(2)]
    sib = at(y, zh, x, 1 - core, col)
    fme = jnp.where(first, y, x)
    lme = jnp.where(first, x, y)
    zof = [(zh + d) % 4 for d in DELTAS]

    feat_in = pltpu.make_async_copy(feat4.at[0], feat_raw, in_sem)
    feat_in.start()
    barrier = pltpu.get_barrier_semaphore()
    for d in far + yn:
        pl.semaphore_signal(barrier, inc=1, device_id=d, device_id_type=MESH)

    def peer(t):
        return (dp, (row + t // 4) % 8, (col + t % 4) % 4)

    def greet(t, _):
        pl.semaphore_signal(barrier, inc=1, device_id=peer(t), device_id_type=MESH)
        return 0

    lax.fori_loop(1, 32, greet, 0)

    isodd = y % 2 == 1
    zero8 = jnp.zeros((8, CH), F32)

    def both(a, b):
        return jnp.where(isodd, b, a)

    def pair(j):
        s, t = weight[2 * j].astype(F32), weight[2 * j + 1].astype(F32)
        a = jnp.concatenate([s, t[32:40], t[0:32]], axis=0)
        b = jnp.concatenate([s[8:40], t[0:8], s[0:8], t[8:40]], axis=0)
        return both(a, b).astype(BF)

    @pl.when(first)
    def _():
        for j in range(4):
            v = pair(j)
            for n in range(3):
                wall[0, zh, j, y, 80 * n : 80 * n + 80, :] = v[:, 128 * n : 128 * n + 128]

    @pl.when(jnp.logical_not(first))
    def _():
        last = weight[8].astype(F32)
        tail = both(
            jnp.concatenate([last, zero8], axis=0), jnp.concatenate([zero8, last], axis=0)
        ).astype(BF)
        for j in range(4):
            v = pair(j)
            for n in range(2):
                wall[1, zh, y, j, 80 * n : 80 * n + 80, :] = v[:, 384 + 128 * n : 512 + 128 * n]
            for s in range(4):
                m = 4 * j + s
                if m < 15:
                    n, r = m // 3, m % 3
                    wall[1, zh, y, j, 160 + 16 * s : 176 + 16 * s, :] = tail[
                        16 * r : 16 * r + 16, 128 * n : 128 * n + 128
                    ]
                else:
                    wall[1, zh, y, j, 160 + 16 * s : 176 + 16 * s, :] = jnp.zeros((16, 128), BF)
            wall[1, zh, y, j, 224:240, :] = jnp.zeros((16, 128), BF)

    def clear(t, _):
        for k in range(4):
            wm[k, t] = jnp.zeros((256, CH), BF)
        return 0

    lax.fori_loop(0, 9, clear, 0)
    pl.semaphore_wait(barrier, 36)

    def copy(src, dst, s, r, d):
        return pltpu.make_async_remote_copy(src, dst, s, r, device_id=d, device_id_type=MESH)

    def zc(i):
        blk = wall.at[core, zh, lme, fme]
        return copy(blk, blk, z_s.at[i], z_r.at[i], far[i])

    def zin(k):
        i = {3: 0, 1: 1, 2: 2}[DELTAS[k]]
        blk = wall.at[core, zof[k], lme, fme]
        return copy(blk, blk, z_s.at[i], z_r.at[i], far[i])

    def fc(k, i, who):
        blk = wall.at[core, zof[k], lme, (fme + who) % 4]
        return copy(blk, blk, f_s.at[k, i], f_r.at[k, i], fdev[i])

    def fhc(k, i, who):
        rows = pl.ds(0, CUT) if i == 0 else pl.ds(CUT, BLK - CUT)
        blk = wall.at[core, zof[k], lme, (fme + who) % 4, rows]
        return copy(blk, blk, fh_s.at[k, i], fh_r.at[k, i], fdev[i])

    def pc(k, e, i, who):
        blk = wall.at[core, zof[k], (lme + who) % 4, (fme + e) % 4]
        return copy(blk, blk, p_s.at[k, e, i], p_r.at[k, e, i], ldev[i])

    def qc(k, e, who):
        blk = wall.at[core, zof[k], (lme + who) % 4, (fme + e) % 4]
        return copy(blk, blk, q_s.at[k, e], q_r.at[k, e], ldev[0 if e < 2 else 1])

    def sc(k, w, which):
        l_there = jnp.where(core == which, lme, jnp.where(first, y, x))
        blk = wall.at[which, zof[k], (l_there + w) % 4]
        return copy(blk, blk, c_s.at[k, w], c_r.at[k, w], sib)

    def f_send(k):
        fc(k, 0, 0).start()
        fc(k, 1, 0).start()

    def f_fwd(k):
        fc(k, 0, 3).wait_recv()
        fhc(k, 0, 3).start()
        fc(k, 1, 1).wait_recv()
        fhc(k, 1, 1).start()

    def f_done(k):
        fhc(k, 0, 2).wait_recv()
        fhc(k, 1, 2).wait_recv()

    def f_sent(k):
        fc(k, 0, 0).wait_send()
        fc(k, 1, 0).wait_send()
        fhc(k, 0, 3).wait_send()
        fhc(k, 1, 1).wait_send()

    def on(k, e, cond_fn):
        if k == 0 and e == 0:
            pl.when(jnp.logical_not(first))(cond_fn)
        else:
            cond_fn()

    def l_send(k, e):
        pc(k, e, 0, 0).start()
        pc(k, e, 1, 0).start()

    def l_fwd(k, *es):
        for e in es:
            def go(e=e):
                i, who = (0, 3) if e < 2 else (1, 1)
                pc(k, e, i, who).wait_recv()
                qc(k, e, who).start()
            on(k, e, go)

    def l_other(k):
        for e in range(4):
            def go(e=e):
                i, who = (1, 1) if e < 2 else (0, 3)
                pc(k, e, i, who).wait_recv()
            on(k, e, go)

    def l_last(k):
        for e in range(4):
            on(k, e, lambda e=e: qc(k, e, 2).wait_recv())

    def l_sent(k):
        for e in range(4):
            def go(e=e):
                pc(k, e, 0, 0).wait_send()
                pc(k, e, 1, 0).wait_send()
                qc(k, e, 3 if e < 2 else 1).wait_send()
            on(k, e, go)

    def s_send(k, *ws):
        for w in ws:
            sc(k, w, core).start()

    def s_wait(k):
        for w in range(4):
            sc(k, w, 1 - core).wait_recv()

    NEAR = (1, 3)
    zc(0).start()
    zc(1).start()

    @pl.when(first)
    def _():
        f_send(0)

    @pl.when(jnp.logical_not(first))
    def _():
        for e in (0, 1, 3, 2):
            l_send(0, e)

    zc(2).start()

    old = lax.broadcasted_iota(jnp.int32, (CH, 128), 0)
    shift_by = jnp.zeros((CH, 128), jnp.int32)
    for i in range(16):
        j = (i % 4) * 4 + i // 4
        shift_by = jnp.where(old >= 40 * i, 40 * (j - i), shift_by)
    target = old + shift_by
    lane0 = lax.broadcasted_iota(jnp.int32, (CH, 128), 1)
    perm = jnp.concatenate(
        [jnp.where(target == lane0 + 128 * n, 1.0, 0.0).astype(BF) for n in range(5)], axis=1
    )

    feat_in.wait()

    def stage(p, _):
        r = 2 * p
        two = jnp.concatenate([feat_raw[r].astype(F32), feat_raw[r + 1].astype(F32)], axis=0)
        feat[p] = two.astype(BF)
        return 0

    lax.fori_loop(0, R // 2, stage, 0)
    def reorder(h, _):
        v = dot(feat[pl.ds(5 * h, 5)].reshape(400, CH), perm)
        acc[pl.ds(pl.multiple_of(400 * h, 400), 400), :] = v
        return 0

    lax.fori_loop(0, 2, reorder, 0)

    def pass1(p, total):
        r = 2 * p
        v = acc[pl.ds(pl.multiple_of(80 * p, 80), 80), :]
        feat[p] = v.astype(BF)
        col_out[0, pl.ds(r, 1), :] = v[0:1]
        col_out[1, pl.ds(r, 1), :] = v[39:40]
        col_out[0, pl.ds(r + 1, 1), :] = v[40:41]
        col_out[1, pl.ds(r + 1, 1), :] = v[79:80]
        for i in range(10):
            total = total + v[8 * i : 8 * i + 8]
        return total

    zeros = jnp.zeros((8, CH), F32)
    col_out[0, 16:24, :] = zeros
    col_out[1, 16:24, :] = zeros
    total = lax.fori_loop(0, R // 2, pass1, zeros)


    halo = [
        (feat.at[R // 2 - 1], row_in.at[0], (dp, down, col)),
        (feat.at[0], row_in.at[1], (dp, up, col)),
        (col_out.at[1], col_in.at[0], (dp, row, right)),
        (col_out.at[0], col_in.at[1], (dp, row, left)),
        (col_out.at[1, pl.ds(16, 8)], cor_in.at[0], (dp, down, right)),
        (col_out.at[0, pl.ds(16, 8)], cor_in.at[1], (dp, down, left)),
        (col_out.at[1, pl.ds(0, 8)], cor_in.at[2], (dp, up, right)),
        (col_out.at[0, pl.ds(0, 8)], cor_in.at[3], (dp, up, left)),
    ]
    around = [
        (dp, down, right), (dp, down, col), (dp, down, left),
        (dp, row, right), (dp, row, left),
        (dp, up, right), (dp, up, col), (dp, up, left),
    ]
    halo += [(mask, mask_in.at[i], d) for i, d in enumerate(around)]
    hcs = [copy(s, d, h_s.at[i], h_r.at[i], dev) for i, (s, d, dev) in enumerate(halo)]
    for c in hcs:
        c.start()

    chan = lax.broadcasted_iota(jnp.int32, (CH, 128), 0)
    lane = lax.broadcasted_iota(jnp.int32, (CH, 128), 1)
    per = CH // GROUPS
    gm = jnp.where((chan >= lane * per) & (chan < lane * per + per), 1.0, 0.0).astype(BF)
    gm = lax.dot_general(perm, gm, (((0,), (0,)), ((), ())), preferred_element_type=F32).astype(BF)
    lane_t = lax.broadcasted_iota(jnp.int32, (128, CH), 0)
    chan_t = lax.broadcasted_iota(jnp.int32, (128, CH), 1)
    gt = jnp.where((chan_t >= lane_t * per) & (chan_t < lane_t * per + per), 1.0, 0.0).astype(BF)
    gt = dot(gt, perm).astype(BF)

    def spread(v):
        return jnp.broadcast_to(jnp.sum(v, axis=0, keepdims=True), v.shape)

    n_here = float(R * C * per)
    mean_here = dot3(spread(total), gm) * (1.0 / n_here)
    mean_chan = dot3(mean_here, gt)[0:1]

    def pass2(p, total):
        d = feat[p].astype(F32) - mean_chan
        d = d * d
        for i in range(10):
            total = total + d[8 * i : 8 * i + 8]
        return total

    m2 = dot3(spread(lax.fori_loop(0, R // 2, pass2, zeros)), gm)
    sub = lax.broadcasted_iota(jnp.int32, (8, 128), 0)
    st_out[...] = jnp.where(sub == 0, mean_here, m2)

    def tc(t):
        return copy(st_out, st_in.at[t], t_s.at[t], t_r.at[t], peer(t))

    def st_send(t, _):
        tc(t).start()
        return 0

    lax.fori_loop(1, 32, st_send, 0)

    @pl.when(first)
    def _():
        f_fwd(0)
        l_send(0, 1)
        l_send(0, 3)
        f_done(0)
        l_send(0, 2)

    s_send(0, 0)
    l_fwd(0, 0)
    zin(1).wait_recv()
    l_send(1, 0)
    f_send(1)
    zin(2).wait_recv()
    l_send(2, 0)
    f_send(2)

    for c in hcs[8:]:
        c.wait_recv()

    lane1 = lax.broadcasted_iota(jnp.int32, (R, 128), 1)

    def wide(v):
        return jnp.concatenate([v.astype(F32), jnp.zeros((R, 128 - C), F32)], axis=1)

    def strip(lef, mid, rig):
        a = pltpu.roll(wide(lef), 128 - 39, 1)
        b = pltpu.roll(wide(mid), 1, 1)
        c = pltpu.roll(wide(rig), 41, 1)
        res = jnp.where((lane1 >= 1) & (lane1 <= 40), b, 0.0)
        res = jnp.where((lane1 == 0) & (col > 0), a, res)
        return jnp.where((lane1 == 41) & (col < 3), c, res)

    above = strip(mask_in[0], mask_in[1], mask_in[2])
    here = strip(mask_in[3], mask[...], mask_in[4])
    below = strip(mask_in[5], mask_in[6], mask_in[7])
    mpad[...] = jnp.zeros((128, 128), F32)
    mpad[0:1, :] = jnp.where(row > 0, above[19:20], 0.0)
    mpad[1:21, :] = here
    mpad[21:22, :] = jnp.where(row < 7, below[0:1], 0.0)
    mcols[...] = mpad[...].T
    d3 = mcols[0:40, :] + pltpu.roll(mcols[1:41, :], 32, 1) + pltpu.roll(mcols[2:42, :], 64, 1)

    def fill_mask(p, _):
        a = pltpu.roll(d3, lax.rem(128 - 2 * p, 128), 1)
        b = pltpu.roll(d3, lax.rem(127 - 2 * p, 128), 1)
        mtaps[pl.ds(pl.multiple_of(80 * p, 80), 80), :] = jnp.concatenate([a, b], axis=0).astype(BF)
        return 0

    lax.fori_loop(0, 10, fill_mask, 0)
    gtab[...] = jnp.zeros((128, CH), F32)
    for dy in range(3):
        for dx in range(3):
            gtab[32 * dx + dy : 32 * dx + dy + 1, :] = mask_w[3 * dy + dx : 3 * dy + dx + 1, :]
    g = gtab[...]
    g_hi = g.astype(BF)
    g_rest = g - g_hi.astype(F32)
    g_mid = g_rest.astype(BF)
    g_low = (g_rest - g_mid.astype(F32)).astype(BF)
    bias_row = bias[...].reshape(1, CH)

    g_all = jnp.concatenate([g_hi, g_mid, g_low], axis=0)

    def mask_term(h, _):
        rows = pl.ds(pl.multiple_of(400 * h, 400), 400)
        m = mtaps[rows, :]
        acc[rows, :] = dot(jnp.concatenate([m, m, m], axis=1), g_all) + bias_row
        return 0

    lax.fori_loop(0, 2, mask_term, 0)

    l_fwd(0, 1, 3, 2)
    f_fwd(1)
    l_send(1, 1)
    l_send(1, 3)
    f_fwd(2)
    l_send(2, 1)
    l_send(2, 3)

    def st_mean(t, total):
        tc(t).wait_recv()
        return total + st_in[t]

    mean_g = lax.fori_loop(1, 32, st_mean, st_out[...])[0:1] * (1.0 / 32.0)

    def st_sq(t, total):
        v = st_in[t]
        dm = v[0:1] - mean_g
        return total + v[1:2] + n_here * dm * dm

    dm = st_out[0:1, :] - mean_g
    sq = lax.fori_loop(1, 32, st_sq, st_out[1:2, :] + n_here * dm * dm)
    rs_g = lax.rsqrt(sq * (1.0 / (32.0 * n_here)) + EPS)
    both_g = dot3(jnp.concatenate([mean_g, rs_g, jnp.zeros((6, 128), F32)], axis=0), gt)
    mean_c, rs_c = both_g[0:1], both_g[1:2]
    gs = jnp.concatenate(
        [gain[...].reshape(1, CH), shift[...].reshape(1, CH), jnp.zeros((6, CH), F32)], axis=0
    )
    gs = dot3(gs, perm)
    gain_c, shift_c = gs[0:1], gs[1:2]

    def activate(v):
        v = (v - mean_c) * rs_c * gain_c + shift_c
        return v / (1.0 + jnp.exp(-v))

    f_done(1)
    l_send(1, 2)
    f_done(2)
    l_send(2, 2)
    l_fwd(1, 0)
    l_fwd(2, 0)
    s_send(1, 0)
    s_send(2, 0)
    l_other(0)
    s_send(0, 1, 3)

    def act_rows(p, _):
        v = activate(feat[p].astype(F32))
        act[2 * p + 1, 8 : 8 + C, :] = v[0:C]
        act[2 * p + 2, 8 : 8 + C, :] = v[C : 2 * C]
        return 0

    lax.fori_loop(0, 5, act_rows, 0)
    l_fwd(1, 1, 3)
    l_fwd(2, 1, 3)
    zin(3).wait_recv()
    l_send(3, 0)
    f_send(3)
    lax.fori_loop(5, 10, act_rows, 0)
    l_last(0)
    s_send(0, 2)
    f_fwd(3)
    l_send(3, 1)
    l_send(3, 3)
    l_fwd(1, 2)
    l_fwd(2, 2)

    for c in hcs[:8]:
        c.wait_recv()
    act[0, 8 : 8 + C, :] = jnp.where(row > 0, activate(row_in[0, 40:80].astype(F32)), 0.0)
    act[21, 8 : 8 + C, :] = jnp.where(row < 7, activate(row_in[1, 0:40].astype(F32)), 0.0)
    for side, there, off in ((0, col > 0, 7), (1, col < 3, 48)):
        edge = jnp.where(there, activate(col_in[side]), 0.0)
        for r in range(R):
            act[r + 1, off : off + 1, :] = edge[r : r + 1]
    for i, (there, pick, r, spot) in enumerate((
        ((row > 0) & (col > 0), 3, 0, 7),
        ((row > 0) & (col < 3), 3, 0, 48),
        ((row < 7) & (col > 0), 0, 21, 7),
        ((row < 7) & (col < 3), 0, 21, 48),
    )):
        corner = jnp.where(there, activate(cor_in[i]), 0.0)
        act[r, spot : spot + 1, :] = corner[pick : pick + 1]

    f_done(3)
    l_send(3, 2)
    s_send(3, 0)
    l_fwd(3, 0)

    def fill(p, _):
            r = jnp.where(p < 11, 2 * p, 2 * p - 21)
            for dx in range(3):
                a = act[r, 7 + dx : 7 + dx + C, :]
                b = act[r + 1, 7 + dx : 7 + dx + C, :]
                v = jnp.concatenate([a, b], axis=0).astype(BF)
                taps[dx, pl.ds(pl.multiple_of(80 * p, 80), 80), :] = v
            return 0

    lax.fori_loop(0, 11, fill, 0)
    l_other(1)
    s_send(1, 1, 3)
    l_other(2)
    s_send(2, 1, 3)
    lax.fori_loop(11, 21, fill, 0)
    l_fwd(3, 1, 3)

    low_half = lax.broadcasted_iota(jnp.int32, (16, 128), 0) < 8

    def delta(k):
        return jnp.where(k == 0, 0, jnp.where(k == 1, 3, jnp.where(k == 2, 1, 2)))

    def merge(k):
        z = lax.rem(zh + delta(k), 4)

        for m in range(2):
            base = pl.multiple_of(32 * z + 80 * m, 16)
            rows = pl.ds(base, 80)
            ya, yb = 2 * m, 2 * m + 1

            def two(j, _):
                for n in range(5):
                    if n < 3:
                        a = wall.at[0, z, j, ya, pl.ds(80 * n, 80)]
                        b = wall.at[0, z, j, yb, pl.ds(80 * n, 80)]
                    else:
                        a = wall.at[1, z, ya, j, pl.ds(80 * (n - 3), 80)]
                        b = wall.at[1, z, yb, j, pl.ds(80 * (n - 3), 80)]
                    a2, b2 = a[32:48, :].astype(F32), b[32:48, :].astype(F32)
                    mid_s = jnp.where(low_half, a2, b2).astype(BF)
                    mid_t = jnp.concatenate([a2[8:16], b2[0:8]], axis=0).astype(BF)
                    ln = pl.ds(128 * n, 128)
                    wm[k, 2 * j, rows, ln] = jnp.concatenate(
                        [a[0:32, :], mid_s, b[0:32, :]], axis=0
                    )
                    wm[k, 2 * j + 1, rows, ln] = jnp.concatenate(
                        [a[48:80, :], mid_t, b[48:80, :]], axis=0
                    )
                return 0

            lax.fori_loop(0, 4, two, 0)

            def tile(y_, n, r):
                i = 3 * n + r
                return wall[1, z, y_, i // 4, pl.ds(160 + 16 * (i % 4), 16), :]

            for n in range(5):
                mid = jnp.where(low_half, tile(ya, n, 2).astype(F32), tile(yb, n, 0).astype(F32))
                wm[k, 8, rows, pl.ds(128 * n, 128)] = jnp.concatenate(
                    [tile(ya, n, 0), tile(ya, n, 1), mid.astype(BF), tile(yb, n, 1), tile(yb, n, 2)],
                    axis=0,
                )

    def conv(k, dy):
        win = pl.ds(pl.multiple_of(128 * lax.rem(zh + delta(k), 4), 128), 256)
        start = pl.multiple_of(jnp.where(dy == 0, 0, jnp.where(dy == 1, 880, 80)), 80)
        parts = [taps[dx, pl.ds(start, R * C), win] for dx in range(3)]
        rhs = wm[k, pl.ds(3 * dy, 3)].reshape(768, CH)
        acc[...] += dot(jnp.concatenate(parts, axis=1), rhs)

    def step(t, _):
        k, dy = t // 3, lax.rem(t, 3)

        def when(there, *fs):
            @pl.when(t == there)
            def _():
                for f in fs:
                    f()

        for kk in range(4):
            when(3 * kk, lambda kk=kk: s_wait(kk))

        @pl.when(dy == 0)
        def _():
            merge(k)

        conv(k, dy)
        when(
            0,
            lambda: l_last(1), lambda: s_send(1, 2), lambda: l_last(2), lambda: s_send(2, 2),
            lambda: l_fwd(3, 2),
        )
        when(2, lambda: l_other(3), lambda: s_send(3, 1, 3))
        when(3, lambda: l_last(3), lambda: s_send(3, 2))
        return 0

    lax.fori_loop(0, 12, step, 0)
    def finish(r, _):
        out4[0, r] = acc[pl.ds(pl.multiple_of(C * r, 8), C), :].astype(BF)
        return 0

    lax.fori_loop(0, R, finish, 0)

    for i in range(3):
        zc(i).wait_send()

    @pl.when(first)
    def _():
        f_sent(0)

    for k in range(1, 4):
        f_sent(k)
    for k in range(4):
        l_sent(k)
        for w in range(4):
            sc(k, w, core).wait_send()
    for c in hcs:
        c.wait_send()

    def st_sent(t, _):
        tc(t).wait_send()
        return 0

    lax.fori_loop(1, 32, st_sent, 0)


def local(features, hole_mask, norm_gain, norm_shift, conv_weight, mask_weight, conv_bias):
    vm = pl.BlockSpec(memory_space=pltpu.VMEM)
    dma = pltpu.SemaphoreType.DMA
    result = pl.pallas_call(
        kernel,
        out_shape=jax.ShapeDtypeStruct((1, R, C, CH), BF),
        in_specs=[pl.BlockSpec(memory_space=pl.ANY)] + [vm] * 6,
        out_specs=vm,
        scratch_shapes=[
            pltpu.VMEM((2, 4, 4, 4, BLK, 128), BF),
            pltpu.VMEM((4, 9, 256, CH), BF),
            pltpu.VMEM((22, STRIDE, CH), F32),
            pltpu.VMEM((3, 42 * C, CH), BF),
            pltpu.VMEM((R * C, CH), F32),
            pltpu.VMEM((R // 2, 2 * C, CH), BF),
            pltpu.VMEM((2, 24, CH), F32),
            pltpu.VMEM((2, 2 * C, CH), BF),
            pltpu.VMEM((2, 24, CH), F32),
            pltpu.VMEM((4, 8, CH), F32),
            pltpu.VMEM((8, R, C), jnp.int32),
            pltpu.VMEM((128, 128), F32),
            pltpu.VMEM((128, 128), F32),
            pltpu.VMEM((R * C, 128), BF),
            pltpu.VMEM((128, CH), F32),
            pltpu.VMEM((8, 128), F32),
            pltpu.VMEM((32, 8, 128), F32),
            dma((3,)), dma((3,)),
            dma((4, 2)), dma((4, 2)), dma((4, 2)), dma((4, 2)),
            dma((4, 4, 2)), dma((4, 4, 2)), dma((4, 4)), dma((4, 4)),
            dma((4, 4)), dma((4, 4)), dma((16,)), dma((16,)), dma((32,)), dma((32,)), dma(()),
            pltpu.VMEM((R, C, CH), BF),
        ],
        compiler_params=pltpu.CompilerParams(
            collective_id=0, has_side_effects=True, vmem_limit_bytes=56 << 20
        ),
        name="conv",
    )(features, hole_mask, norm_gain, norm_shift, conv_weight, mask_weight, conv_bias)
    return result


def solution(mesh):
    image = P("dp", "row", "col", None)
    return jax.shard_map(
        local,
        mesh=mesh,
        in_specs=(image, P("dp", "row", "col"), P(), P(), P(None, "dp", None), P(), P()),
        out_specs=image,
        check_vma=False,
    )
```

```python
import jax
import jax.numpy as jnp
from jax import lax
from jax.experimental import pallas as pl
from jax.experimental.pallas import tpu as pltpu
from jax.sharding import PartitionSpec as P

GROUPS = 32
EPS = 1e-05
MESH = pl.DeviceIdType.MESH
BF = jnp.bfloat16
F32 = jnp.float32
R, C, CH = 20, 40, 640
BLK = 240
CUT = 128
STRIDE = 56
DELTAS = (0, 3, 1, 2)


def dot(a, b):
    return jnp.dot(a, b, preferred_element_type=F32)


def dot3(a, b):
    hi = a.astype(BF)
    rest = a - hi.astype(F32)
    mid = rest.astype(BF)
    low = (rest - mid.astype(F32)).astype(BF)
    return dot(hi, b) + dot(mid, b) + dot(low, b)


def kernel(
    feat4, mask3, gain, shift, weight, mask_w, bias, out4,
    wall, wm, act, taps, acc, mask, feat, col_out, row_in, col_in, cor_in,
    mask_in, mpad, mcols, mtaps, gtab, st_out, st_in,
    w_s, z_r, f_r, fh_r, p_r, q_r, c_r, h_s, h_r, m_r, t_s, t_r, in_sem, feat_raw,
):
    dp, row, col = lax.axis_index("dp"), lax.axis_index("row"), lax.axis_index("col")
    x, core = row // 2, row % 2
    y, zh = dp // 4, dp % 4

    def at(y_, zh_, x_, core_, col_):
        return (y_ * 4 + zh_, x_ * 2 + core_, col_)

    up, down = (row + 7) % 8, (row + 1) % 8
    left, right = (col + 3) % 4, (col + 1) % 4
    far = [at(y, (zh + s) % 4, x, core, col) for s in (1, 3, 2)]
    xn = [at(y, zh, (x + 1) % 4, core, col), at(y, zh, (x + 3) % 4, core, col)]
    yn = [at((y + 1) % 4, zh, x, core, col), at((y + 3) % 4, zh, x, core, col)]
    first = core == 0
    fdev = [tuple(jnp.where(first, a, b) for a, b in zip(yn[i], xn[i])) for i in range(2)]
    ldev = [tuple(jnp.where(first, b, a) for a, b in zip(yn[i], xn[i])) for i in range(2)]
    sib = at(y, zh, x, 1 - core, col)
    fme = jnp.where(first, y, x)
    lme = jnp.where(first, x, y)
    zof = [(zh + d) % 4 for d in DELTAS]

    feat_in = pltpu.make_async_copy(feat4.at[0], feat_raw, in_sem)
    feat_in.start()
    barrier = pltpu.get_barrier_semaphore()
    for d in far + yn:
        pl.semaphore_signal(barrier, inc=1, device_id=d, device_id_type=MESH)

    def peer(t):
        return (dp, (row + t // 4) % 8, (col + t % 4) % 4)

    def greet(t, _):
        pl.semaphore_signal(barrier, inc=1, device_id=peer(t), device_id_type=MESH)
        return 0

    lax.fori_loop(1, 32, greet, 0)

    for r in range(R):
        mask[r : r + 1, :] = mask3[r]

    isodd = y % 2 == 1
    zero8 = jnp.zeros((8, CH), F32)

    def both(a, b):
        return jnp.where(isodd, b, a)

    def pair(j):
        s, t = weight[2 * j].astype(F32), weight[2 * j + 1].astype(F32)
        a = jnp.concatenate([s, t[32:40], t[0:32]], axis=0)
        b = jnp.concatenate([s[8:40], t[0:8], s[0:8], t[8:40]], axis=0)
        return both(a, b).astype(BF)

    @pl.when(first)
    def _():
        for j in range(4):
            v = pair(j)
            for n in range(3):
                wall[0, zh, j, y, 80 * n : 80 * n + 80, :] = v[:, 128 * n : 128 * n + 128]

    @pl.when(jnp.logical_not(first))
    def _():
        last = weight[8].astype(F32)
        tail = both(
            jnp.concatenate([last, zero8], axis=0), jnp.concatenate([zero8, last], axis=0)
        ).astype(BF)
        for j in range(4):
            v = pair(j)
            for n in range(2):
                wall[1, zh, y, j, 80 * n : 80 * n + 80, :] = v[:, 384 + 128 * n : 512 + 128 * n]
            for s in range(4):
                m = 4 * j + s
                if m < 15:
                    n, r = m // 3, m % 3
                    wall[1, zh, y, j, 160 + 16 * s : 176 + 16 * s, :] = tail[
                        16 * r : 16 * r + 16, 128 * n : 128 * n + 128
                    ]
                else:
                    wall[1, zh, y, j, 160 + 16 * s : 176 + 16 * s, :] = jnp.zeros((16, 128), BF)
            wall[1, zh, y, j, 224:240, :] = jnp.zeros((16, 128), BF)

    def clear(t, _):
        for k in range(4):
            wm[k, t] = jnp.zeros((256, CH), BF)
        return 0

    lax.fori_loop(0, 9, clear, 0)
    pl.semaphore_wait(barrier, 36)

    def copy(src, dst, s, r, d):
        return pltpu.make_async_remote_copy(src, dst, s, r, device_id=d, device_id_type=MESH)

    def zc(i):
        blk = wall.at[core, zh, lme, fme]
        return copy(blk, blk, w_s, z_r.at[i], far[i])

    def zin(k):
        i = {3: 0, 1: 1, 2: 2}[DELTAS[k]]
        blk = wall.at[core, zof[k], lme, fme]
        return copy(blk, blk, w_s, z_r.at[i], far[i])

    def fc(k, i, who):
        blk = wall.at[core, zof[k], lme, (fme + who) % 4]
        return copy(blk, blk, w_s, f_r.at[k, i], fdev[i])

    def fhc(k, i, who):
        rows = pl.ds(0, CUT) if i == 0 else pl.ds(CUT, BLK - CUT)
        blk = wall.at[core, zof[k], lme, (fme + who) % 4, rows]
        return copy(blk, blk, w_s, fh_r.at[k, i], fdev[i])

    def pc(k, e, i, who):
        blk = wall.at[core, zof[k], (lme + who) % 4, (fme + e) % 4]
        return copy(blk, blk, w_s, p_r.at[k, e, i], ldev[i])

    def qc(k, e, who):
        blk = wall.at[core, zof[k], (lme + who) % 4, (fme + e) % 4]
        return copy(blk, blk, w_s, q_r.at[k, e], ldev[0 if e < 2 else 1])

    def sc(k, w, which):
        l_there = jnp.where(core == which, lme, jnp.where(first, y, x))
        blk = wall.at[which, zof[k], (l_there + w) % 4]
        return copy(blk, blk, w_s, c_r.at[k], sib)

    def f_send(k):
        fc(k, 0, 0).start()
        fc(k, 1, 0).start()

    def f_fwd(k):
        fc(k, 0, 3).wait_recv()
        fhc(k, 0, 3).start()
        fc(k, 1, 1).wait_recv()
        fhc(k, 1, 1).start()

    def f_done(k):
        fhc(k, 0, 2).wait_recv()
        fhc(k, 1, 2).wait_recv()

    def on(k, e, cond_fn):
        if k == 0 and e == 0:
            pl.when(jnp.logical_not(first))(cond_fn)
        else:
            cond_fn()

    def l_send(k, e):
        pc(k, e, 0, 0).start()
        pc(k, e, 1, 0).start()

    def l_fwd(k, *es):
        for e in es:
            def go(e=e):
                i, who = (0, 3) if e < 2 else (1, 1)
                pc(k, e, i, who).wait_recv()
                qc(k, e, who).start()
            on(k, e, go)

    def l_other(k):
        for e in range(4):
            def go(e=e):
                i, who = (1, 1) if e < 2 else (0, 3)
                pc(k, e, i, who).wait_recv()
            on(k, e, go)

    def l_last(k):
        for e in range(4):
            on(k, e, lambda e=e: qc(k, e, 2).wait_recv())

    def s_send(k, *ws):
        for w in ws:
            sc(k, w, core).start()

    def s_wait(k):
        blk = wall.at[1 - core, zof[k]]
        copy(blk, blk, w_s, c_r.at[k], sib).wait_recv()

    zc(0).start()
    zc(1).start()

    @pl.when(first)
    def _():
        f_send(0)

    @pl.when(jnp.logical_not(first))
    def _():
        for e in (0, 1, 3, 2):
            l_send(0, e)

    zc(2).start()

    old = lax.broadcasted_iota(jnp.int32, (CH, 128), 0)
    shift_by = jnp.zeros((CH, 128), jnp.int32)
    for i in range(16):
        j = (i % 4) * 4 + i // 4
        shift_by = jnp.where(old >= 40 * i, 40 * (j - i), shift_by)
    target = old + shift_by
    lane0 = lax.broadcasted_iota(jnp.int32, (CH, 128), 1)
    perm = jnp.concatenate(
        [jnp.where(target == lane0 + 128 * n, 1.0, 0.0).astype(BF) for n in range(5)], axis=1
    )

    feat_in.wait()

    def stage(p, _):
        r = 2 * p
        two = jnp.concatenate([feat_raw[r].astype(F32), feat_raw[r + 1].astype(F32)], axis=0)
        feat[p] = two.astype(BF)
        return 0

    lax.fori_loop(0, R // 2, stage, 0)
    def reorder(h, _):
        v = dot(feat[pl.ds(5 * h, 5)].reshape(400, CH), perm)
        acc[pl.ds(pl.multiple_of(400 * h, 400), 400), :] = v
        return 0

    lax.fori_loop(0, 2, reorder, 0)

    @pl.when(first)
    def _():
        f_fwd(0)
        l_send(0, 1)
        l_send(0, 3)

    l_fwd(0, 0)

    def pass1(p, total):
        r = 2 * p
        v = acc[pl.ds(pl.multiple_of(80 * p, 80), 80), :]
        feat[p] = v.astype(BF)
        col_out[0, pl.ds(r, 1), :] = v[0:1]
        col_out[1, pl.ds(r, 1), :] = v[39:40]
        col_out[0, pl.ds(r + 1, 1), :] = v[40:41]
        col_out[1, pl.ds(r + 1, 1), :] = v[79:80]
        for i in range(10):
            total = total + v[8 * i : 8 * i + 8]
        return total

    zeros = jnp.zeros((8, CH), F32)
    col_out[0, 16:24, :] = zeros
    col_out[1, 16:24, :] = zeros
    total = lax.fori_loop(0, R // 2, pass1, zeros)

    @pl.when(first)
    def _():
        f_done(0)
        l_send(0, 2)

    s_send(0, 0)


    halo = [
        (feat.at[R // 2 - 1], row_in.at[0], (dp, down, col)),
        (feat.at[0], row_in.at[1], (dp, up, col)),
        (col_out.at[1], col_in.at[0], (dp, row, right)),
        (col_out.at[0], col_in.at[1], (dp, row, left)),
        (col_out.at[1, pl.ds(16, 8)], cor_in.at[0], (dp, down, right)),
        (col_out.at[0, pl.ds(16, 8)], cor_in.at[1], (dp, down, left)),
        (col_out.at[1, pl.ds(0, 8)], cor_in.at[2], (dp, up, right)),
        (col_out.at[0, pl.ds(0, 8)], cor_in.at[3], (dp, up, left)),
    ]
    around = [
        (dp, down, right), (dp, down, col), (dp, down, left),
        (dp, row, right), (dp, row, left),
        (dp, up, right), (dp, up, col), (dp, up, left),
    ]
    halo += [(mask, mask_in.at[i], d) for i, d in enumerate(around)]
    hcs = [
        copy(s, d, h_s.at[i], h_r.at[i] if i < 8 else m_r, dev)
        for i, (s, d, dev) in enumerate(halo)
    ]
    for c in hcs:
        c.start()

    chan = lax.broadcasted_iota(jnp.int32, (CH, 128), 0)
    lane = lax.broadcasted_iota(jnp.int32, (CH, 128), 1)
    per = CH // GROUPS
    gm = jnp.where((chan >= lane * per) & (chan < lane * per + per), 1.0, 0.0).astype(BF)
    gm = lax.dot_general(perm, gm, (((0,), (0,)), ((), ())), preferred_element_type=F32).astype(BF)
    lane_t = lax.broadcasted_iota(jnp.int32, (128, CH), 0)
    chan_t = lax.broadcasted_iota(jnp.int32, (128, CH), 1)
    gt = jnp.where((chan_t >= lane_t * per) & (chan_t < lane_t * per + per), 1.0, 0.0).astype(BF)
    gt = dot(gt, perm).astype(BF)

    def spread(v):
        return jnp.broadcast_to(jnp.sum(v, axis=0, keepdims=True), v.shape)

    n_here = float(R * C * per)
    mean_here = dot3(spread(total), gm) * (1.0 / n_here)
    mean_chan = dot3(mean_here, gt)[0:1]

    def pass2(p, total):
        d = feat[p].astype(F32) - mean_chan
        d = d * d
        for i in range(10):
            total = total + d[8 * i : 8 * i + 8]
        return total

    m2 = dot3(spread(lax.fori_loop(0, R // 2, pass2, zeros)), gm)
    sub = lax.broadcasted_iota(jnp.int32, (8, 128), 0)
    st_out[...] = jnp.where(sub == 0, mean_here, m2)

    def tc(t):
        return copy(st_out, st_in.at[t], t_s, t_r, peer(t))

    def st_send(t, _):
        tc(t).start()
        return 0

    lax.fori_loop(1, 32, st_send, 0)

    zin(1).wait_recv()
    l_send(1, 0)
    f_send(1)
    zin(2).wait_recv()
    l_send(2, 0)
    f_send(2)
    l_fwd(0, 1, 3)

    copy(mask_in, mask_in, h_s.at[0], m_r, sib).wait_recv()

    lane1 = lax.broadcasted_iota(jnp.int32, (R, 128), 1)

    def wide(v):
        return jnp.concatenate([v.astype(F32), jnp.zeros((R, 128 - C), F32)], axis=1)

    def strip(lef, mid, rig):
        a = pltpu.roll(wide(lef), 128 - 39, 1)
        b = pltpu.roll(wide(mid), 1, 1)
        c = pltpu.roll(wide(rig), 41, 1)
        res = jnp.where((lane1 >= 1) & (lane1 <= 40), b, 0.0)
        res = jnp.where((lane1 == 0) & (col > 0), a, res)
        return jnp.where((lane1 == 41) & (col < 3), c, res)

    above = strip(mask_in[0], mask_in[1], mask_in[2])
    here = strip(mask_in[3], mask[...], mask_in[4])
    below = strip(mask_in[5], mask_in[6], mask_in[7])
    mpad[...] = jnp.zeros((128, 128), F32)
    mpad[0:1, :] = jnp.where(row > 0, above[19:20], 0.0)
    mpad[1:21, :] = here
    mpad[21:22, :] = jnp.where(row < 7, below[0:1], 0.0)
    mcols[...] = mpad[...].T
    d3 = mcols[0:40, :] + pltpu.roll(mcols[1:41, :], 32, 1) + pltpu.roll(mcols[2:42, :], 64, 1)

    def fill_mask(p, _):
        a = pltpu.roll(d3, lax.rem(128 - 2 * p, 128), 1)
        b = pltpu.roll(d3, lax.rem(127 - 2 * p, 128), 1)
        mtaps[pl.ds(pl.multiple_of(80 * p, 80), 80), :] = jnp.concatenate([a, b], axis=0).astype(BF)
        return 0

    lax.fori_loop(0, 10, fill_mask, 0)
    gtab[...] = jnp.zeros((128, CH), F32)
    for dy in range(3):
        for dx in range(3):
            gtab[32 * dx + dy : 32 * dx + dy + 1, :] = mask_w[3 * dy + dx : 3 * dy + dx + 1, :]
    g = gtab[...]
    g_hi = g.astype(BF)
    g_rest = g - g_hi.astype(F32)
    g_mid = g_rest.astype(BF)
    g_low = (g_rest - g_mid.astype(F32)).astype(BF)
    bias_row = bias[...].reshape(1, CH)

    g_all = jnp.concatenate([g_hi, g_mid, g_low], axis=0)

    def mask_term(h, _):
        rows = pl.ds(pl.multiple_of(400 * h, 400), 400)
        m = mtaps[rows, :]
        acc[rows, :] = dot(jnp.concatenate([m, m, m], axis=1), g_all) + bias_row
        return 0

    lax.fori_loop(0, 2, mask_term, 0)

    f_fwd(1)
    l_send(1, 1)
    l_send(1, 3)
    f_fwd(2)
    l_send(2, 1)
    l_send(2, 3)
    l_fwd(0, 2)
    l_fwd(1, 0)
    l_fwd(2, 0)

    copy(st_in.at[pl.ds(1, 31)], st_in.at[pl.ds(1, 31)], t_s, t_r, sib).wait_recv()

    def st_mean(t, total):
        return total + st_in[t]

    mean_g = lax.fori_loop(1, 32, st_mean, st_out[...])[0:1] * (1.0 / 32.0)

    def st_sq(t, total):
        v = st_in[t]
        dm = v[0:1] - mean_g
        return total + v[1:2] + n_here * dm * dm

    dm = st_out[0:1, :] - mean_g
    sq = lax.fori_loop(1, 32, st_sq, st_out[1:2, :] + n_here * dm * dm)
    rs_g = lax.rsqrt(sq * (1.0 / (32.0 * n_here)) + EPS)
    both_g = dot3(jnp.concatenate([mean_g, rs_g, jnp.zeros((6, 128), F32)], axis=0), gt)
    mean_c, rs_c = both_g[0:1], both_g[1:2]
    gs = jnp.concatenate(
        [gain[...].reshape(1, CH), shift[...].reshape(1, CH), jnp.zeros((6, CH), F32)], axis=0
    )
    gs = dot3(gs, perm)
    gain_c, shift_c = gs[0:1], gs[1:2]

    def activate(v):
        v = (v - mean_c) * rs_c * gain_c + shift_c
        return v / (1.0 + jnp.exp(-v))

    def act_rows(p, _):
        v = activate(feat[p].astype(F32))
        act[2 * p + 1, 8 : 8 + C, :] = v[0:C]
        act[2 * p + 2, 8 : 8 + C, :] = v[C : 2 * C]
        return 0

    f_done(1)
    l_send(1, 2)
    f_done(2)
    l_send(2, 2)
    lax.fori_loop(0, 5, act_rows, 0)
    zin(3).wait_recv()
    l_send(3, 0)
    f_send(3)
    s_send(1, 0)
    s_send(2, 0)
    l_fwd(1, 1, 3)
    l_fwd(2, 1, 3)
    l_other(0)
    s_send(0, 1, 3)
    lax.fori_loop(5, 10, act_rows, 0)
    f_fwd(3)
    l_send(3, 1)
    l_send(3, 3)
    l_last(0)
    s_send(0, 2)
    l_fwd(1, 2)
    l_fwd(2, 2)

    for c in hcs[:8]:
        c.wait_recv()
    act[0, 8 : 8 + C, :] = jnp.where(row > 0, activate(row_in[0, 40:80].astype(F32)), 0.0)
    act[21, 8 : 8 + C, :] = jnp.where(row < 7, activate(row_in[1, 0:40].astype(F32)), 0.0)
    for side, there, off in ((0, col > 0, 7), (1, col < 3, 48)):
        edge = jnp.where(there, activate(col_in[side]), 0.0)
        for r in range(R):
            act[r + 1, off : off + 1, :] = edge[r : r + 1]
    for i, (there, pick, r, spot) in enumerate((
        ((row > 0) & (col > 0), 3, 0, 7),
        ((row > 0) & (col < 3), 3, 0, 48),
        ((row < 7) & (col > 0), 0, 21, 7),
        ((row < 7) & (col < 3), 0, 21, 48),
    )):
        corner = jnp.where(there, activate(cor_in[i]), 0.0)
        act[r, spot : spot + 1, :] = corner[pick : pick + 1]

    f_done(3)
    l_send(3, 2)
    s_send(3, 0)
    l_fwd(3, 0)

    def fill(p, _):
            r = jnp.where(p < 11, 2 * p, 2 * p - 21)
            for dx in range(3):
                a = act[r, 7 + dx : 7 + dx + C, :]
                b = act[r + 1, 7 + dx : 7 + dx + C, :]
                v = jnp.concatenate([a, b], axis=0).astype(BF)
                taps[dx, pl.ds(pl.multiple_of(80 * p, 80), 80), :] = v
            return 0

    lax.fori_loop(0, 11, fill, 0)
    l_other(1)
    s_send(1, 1, 3)
    l_other(2)
    s_send(2, 1, 3)
    lax.fori_loop(11, 21, fill, 0)
    l_fwd(3, 1, 3)

    low_half = lax.broadcasted_iota(jnp.int32, (16, 128), 0) < 8

    def delta(k):
        return jnp.where(k == 0, 0, jnp.where(k == 1, 3, jnp.where(k == 2, 1, 2)))

    def merge(k):
        z = lax.rem(zh + delta(k), 4)

        for m in range(2):
            base = pl.multiple_of(32 * z + 80 * m, 16)
            rows = pl.ds(base, 80)
            ya, yb = 2 * m, 2 * m + 1

            def two(j, _):
                for n in range(5):
                    if n < 3:
                        a = wall.at[0, z, j, ya, pl.ds(80 * n, 80)]
                        b = wall.at[0, z, j, yb, pl.ds(80 * n, 80)]
                    else:
                        a = wall.at[1, z, ya, j, pl.ds(80 * (n - 3), 80)]
                        b = wall.at[1, z, yb, j, pl.ds(80 * (n - 3), 80)]
                    a2, b2 = a[32:48, :].astype(F32), b[32:48, :].astype(F32)
                    mid_s = jnp.where(low_half, a2, b2).astype(BF)
                    mid_t = jnp.concatenate([a2[8:16], b2[0:8]], axis=0).astype(BF)
                    ln = pl.ds(128 * n, 128)
                    wm[k, 2 * j, rows, ln] = jnp.concatenate(
                        [a[0:32, :], mid_s, b[0:32, :]], axis=0
                    )
                    wm[k, 2 * j + 1, rows, ln] = jnp.concatenate(
                        [a[48:80, :], mid_t, b[48:80, :]], axis=0
                    )
                return 0

            lax.fori_loop(0, 4, two, 0)

            def tile(y_, n, r):
                i = 3 * n + r
                return wall[1, z, y_, i // 4, pl.ds(160 + 16 * (i % 4), 16), :]

            for n in range(5):
                mid = jnp.where(low_half, tile(ya, n, 2).astype(F32), tile(yb, n, 0).astype(F32))
                wm[k, 8, rows, pl.ds(128 * n, 128)] = jnp.concatenate(
                    [tile(ya, n, 0), tile(ya, n, 1), mid.astype(BF), tile(yb, n, 1), tile(yb, n, 2)],
                    axis=0,
                )

    def conv(k, dy):
        win = pl.ds(pl.multiple_of(128 * lax.rem(zh + delta(k), 4), 128), 256)
        start = pl.multiple_of(jnp.where(dy == 0, 0, jnp.where(dy == 1, 880, 80)), 80)
        parts = [taps[dx, pl.ds(start, R * C), win] for dx in range(3)]
        rhs = wm[k, pl.ds(3 * dy, 3)].reshape(768, CH)
        acc[...] += dot(jnp.concatenate(parts, axis=1), rhs)

    def step(t, _):
        k, dy = t // 3, lax.rem(t, 3)

        def when(there, *fs):
            @pl.when(t == there)
            def _():
                for f in fs:
                    f()

        for kk in range(4):
            when(3 * kk, lambda kk=kk: s_wait(kk))

        @pl.when(dy == 0)
        def _():
            merge(k)

        conv(k, dy)
        when(
            0,
            lambda: l_last(1), lambda: s_send(1, 2), lambda: l_last(2), lambda: s_send(2, 2),
            lambda: l_fwd(3, 2),
        )
        when(2, lambda: l_other(3), lambda: s_send(3, 1, 3))
        when(3, lambda: l_last(3), lambda: s_send(3, 2))
        return 0

    lax.fori_loop(0, 12, step, 0)
    def finish(r, _):
        out4[0, r] = acc[pl.ds(pl.multiple_of(C * r, 8), C), :].astype(BF)
        return 0

    lax.fori_loop(0, R, finish, 0)

    for blk in (wall.at[0], wall.at[1, pl.ds(0, 3)], wall.at[1, 3, pl.ds(0, 3)]):
        copy(blk, blk, w_s, z_r.at[0], sib).wait_send()
    for c in hcs:
        c.wait_send()
    copy(st_in.at[pl.ds(1, 31)], st_in.at[pl.ds(1, 31)], t_s, t_r, sib).wait_send()


def local(features, hole_mask, norm_gain, norm_shift, conv_weight, mask_weight, conv_bias):
    vm = pl.BlockSpec(memory_space=pltpu.VMEM)
    dma = pltpu.SemaphoreType.DMA
    result = pl.pallas_call(
        kernel,
        out_shape=jax.ShapeDtypeStruct((1, R, C, CH), BF),
        in_specs=[pl.BlockSpec(memory_space=pl.ANY)] + [vm] * 6,
        out_specs=vm,
        scratch_shapes=[
            pltpu.VMEM((2, 4, 4, 4, BLK, 128), BF),
            pltpu.VMEM((4, 9, 256, CH), BF),
            pltpu.VMEM((22, STRIDE, CH), F32),
            pltpu.VMEM((3, 42 * C, CH), BF),
            pltpu.VMEM((R * C, CH), F32),
            pltpu.VMEM((R, C), jnp.int32),
            pltpu.VMEM((R // 2, 2 * C, CH), BF),
            pltpu.VMEM((2, 24, CH), F32),
            pltpu.VMEM((2, 2 * C, CH), BF),
            pltpu.VMEM((2, 24, CH), F32),
            pltpu.VMEM((4, 8, CH), F32),
            pltpu.VMEM((8, R, C), jnp.int32),
            pltpu.VMEM((128, 128), F32),
            pltpu.VMEM((128, 128), F32),
            pltpu.VMEM((R * C, 128), BF),
            pltpu.VMEM((128, CH), F32),
            pltpu.VMEM((8, 128), F32),
            pltpu.VMEM((32, 8, 128), F32),
            dma(()), dma((3,)), dma((4, 2)), dma((4, 2)), dma((4, 4, 2)), dma((4, 4)), dma((4,)),
            dma((16,)), dma((8,)), dma(()), dma(()), dma(()), dma(()),
            pltpu.VMEM((R, C, CH), BF),
        ],
        compiler_params=pltpu.CompilerParams(
            collective_id=0, has_side_effects=True, vmem_limit_bytes=56 << 20
        ),
        name="conv",
    )(features, hole_mask.reshape(R, 1, C), norm_gain, norm_shift, conv_weight, mask_weight, conv_bias)
    return result


def solution(mesh):
    image = P("dp", "row", "col", None)
    return jax.shard_map(
        local,
        mesh=mesh,
        in_specs=(image, P("dp", "row", "col"), P(), P(), P(None, "dp", None), P(), P()),
        out_specs=image,
        check_vma=False,
    )
```

```python
import jax
import jax.numpy as jnp
from jax import lax
from jax.experimental import pallas as pl
from jax.experimental.pallas import tpu as pltpu
from jax.sharding import PartitionSpec as P

GROUPS = 32
EPS = 1e-05
MESH = pl.DeviceIdType.MESH
BF = jnp.bfloat16
F32 = jnp.float32
R, C, CH = 20, 40, 640
BLK = 240
CUT = 128
STRIDE = 56
DELTAS = (0, 3, 1, 2)
DIRECT = (1, 2, 3)


def dot(a, b):
    return jnp.dot(a, b, preferred_element_type=F32)


def dot3(a, b):
    hi = a.astype(BF)
    rest = a - hi.astype(F32)
    mid = rest.astype(BF)
    low = (rest - mid.astype(F32)).astype(BF)
    return dot(hi, b) + dot(mid, b) + dot(low, b)


def kernel(
    feat4, mask3, gain, shift, weight, mask_w, bias, out4,
    wall, wm, act, taps, acc, mask, feat, col_out, row_in, col_in, cor_in,
    mask_in, mpad, mcols, mtaps, gtab, st_out, st_in,
    w_s, z_r, f_r, fh_r, p_r, q_r, c_r, h_s, h_r, m_r, t_s, t_r, in_sem, feat_raw,
):
    dp, row, col = lax.axis_index("dp"), lax.axis_index("row"), lax.axis_index("col")
    x, core = row // 2, row % 2
    y, zh = dp // 4, dp % 4

    def at(y_, zh_, x_, core_, col_):
        return (y_ * 4 + zh_, x_ * 2 + core_, col_)

    up, down = (row + 7) % 8, (row + 1) % 8
    left, right = (col + 3) % 4, (col + 1) % 4
    far = [at(y, (zh + s) % 4, x, core, col) for s in (1, 3, 2)]
    xn = [at(y, zh, (x + 1) % 4, core, col), at(y, zh, (x + 3) % 4, core, col)]
    yn = [at((y + 1) % 4, zh, x, core, col), at((y + 3) % 4, zh, x, core, col)]
    first = core == 0
    fdev = [tuple(jnp.where(first, a, b) for a, b in zip(yn[i], xn[i])) for i in range(2)]
    ldev = [tuple(jnp.where(first, b, a) for a, b in zip(yn[i], xn[i])) for i in range(2)]
    sib = at(y, zh, x, 1 - core, col)
    fme = jnp.where(first, y, x)
    lme = jnp.where(first, x, y)
    zof = [(zh + d) % 4 for d in DELTAS]

    feat_in = pltpu.make_async_copy(feat4.at[0], feat_raw, in_sem)
    feat_in.start()
    barrier = pltpu.get_barrier_semaphore()
    x2, y2 = at(y, zh, (x + 2) % 4, core, col), at((y + 2) % 4, zh, x, core, col)
    f2 = tuple(jnp.where(first, a, b) for a, b in zip(y2, x2))
    l2 = tuple(jnp.where(first, b, a) for a, b in zip(y2, x2))
    for d in far + yn + [y2]:
        pl.semaphore_signal(barrier, inc=1, device_id=d, device_id_type=MESH)

    def peer(t):
        return (dp, (row + t // 4) % 8, (col + t % 4) % 4)

    def greet(t, _):
        pl.semaphore_signal(barrier, inc=1, device_id=peer(t), device_id_type=MESH)
        return 0

    lax.fori_loop(1, 32, greet, 0)

    for r in range(R):
        mask[r : r + 1, :] = mask3[r]

    isodd = y % 2 == 1
    zero8 = jnp.zeros((8, CH), F32)

    def both(a, b):
        return jnp.where(isodd, b, a)

    def pair(j):
        s, t = weight[2 * j].astype(F32), weight[2 * j + 1].astype(F32)
        a = jnp.concatenate([s, t[32:40], t[0:32]], axis=0)
        b = jnp.concatenate([s[8:40], t[0:8], s[0:8], t[8:40]], axis=0)
        return both(a, b).astype(BF)

    @pl.when(first)
    def _():
        for j in range(4):
            v = pair(j)
            for n in range(3):
                wall[0, zh, j, y, 80 * n : 80 * n + 80, :] = v[:, 128 * n : 128 * n + 128]

    @pl.when(jnp.logical_not(first))
    def _():
        last = weight[8].astype(F32)
        tail = both(
            jnp.concatenate([last, zero8], axis=0), jnp.concatenate([zero8, last], axis=0)
        ).astype(BF)
        for j in range(4):
            v = pair(j)
            for n in range(2):
                wall[1, zh, y, j, 80 * n : 80 * n + 80, :] = v[:, 384 + 128 * n : 512 + 128 * n]
            for s in range(4):
                m = 4 * j + s
                if m < 15:
                    n, r = m // 3, m % 3
                    wall[1, zh, y, j, 160 + 16 * s : 176 + 16 * s, :] = tail[
                        16 * r : 16 * r + 16, 128 * n : 128 * n + 128
                    ]
                else:
                    wall[1, zh, y, j, 160 + 16 * s : 176 + 16 * s, :] = jnp.zeros((16, 128), BF)
            wall[1, zh, y, j, 224:240, :] = jnp.zeros((16, 128), BF)

    def clear(t, _):
        wm[t, 160:288] = jnp.zeros((128, CH), BF)
        return 0

    lax.fori_loop(0, 9, clear, 0)
    pl.semaphore_wait(barrier, 37)

    def copy(src, dst, s, r, d):
        return pltpu.make_async_remote_copy(src, dst, s, r, device_id=d, device_id_type=MESH)

    def zc(i):
        blk = wall.at[core, zh, lme, fme]
        return copy(blk, blk, w_s, z_r.at[i], far[i])

    def zin(k):
        i = {3: 0, 1: 1, 2: 2}[DELTAS[k]]
        blk = wall.at[core, zof[k], lme, fme]
        return copy(blk, blk, w_s, z_r.at[i], far[i])

    def fc(k, i, who):
        blk = wall.at[core, zof[k], lme, (fme + who) % 4]
        return copy(blk, blk, w_s, f_r.at[k, i], fdev[i])

    def fhc(k, i, who):
        rows = pl.ds(0, CUT) if i == 0 else pl.ds(CUT, BLK - CUT)
        blk = wall.at[core, zof[k], lme, (fme + who) % 4, rows]
        return copy(blk, blk, w_s, fh_r.at[k, i], fdev[i])

    def pc(k, e, i, who):
        blk = wall.at[core, zof[k], (lme + who) % 4, (fme + e) % 4]
        return copy(blk, blk, w_s, p_r.at[k, e, i], ldev[i])

    def qc(k, e, who):
        blk = wall.at[core, zof[k], (lme + who) % 4, (fme + e) % 4]
        return copy(blk, blk, w_s, q_r.at[k, e], ldev[0 if e < 2 else 1])

    def sc(k, w, which):
        l_there = jnp.where(core == which, lme, jnp.where(first, y, x))
        blk = wall.at[which, zof[k], (l_there + w) % 4]
        return copy(blk, blk, w_s, c_r.at[k], sib)

    def f2c(k, who):
        blk = wall.at[core, zof[k], lme, (fme + who) % 4]
        return copy(blk, blk, w_s, fh_r.at[k, 0], f2)

    def l2c(k, e, who):
        blk = wall.at[core, zof[k], (lme + who) % 4, (fme + e) % 4]
        return copy(blk, blk, w_s, q_r.at[k, e], l2)

    def f_send(k):
        fc(k, 0, 0).start()
        fc(k, 1, 0).start()
        if k in DIRECT:
            f2c(k, 0).start()

    def f_fwd(k):
        fc(k, 0, 3).wait_recv()
        if k not in DIRECT:
            fhc(k, 0, 3).start()
        fc(k, 1, 1).wait_recv()
        if k not in DIRECT:
            fhc(k, 1, 1).start()

    def f_done(k):
        if k in DIRECT:
            f2c(k, 2).wait_recv()
        else:
            fhc(k, 0, 2).wait_recv()
            fhc(k, 1, 2).wait_recv()

    def on(k, e, cond_fn):
        if k == 0 and e == 0:
            pl.when(jnp.logical_not(first))(cond_fn)
        else:
            cond_fn()

    def l_send(k, e):
        pc(k, e, 0, 0).start()
        pc(k, e, 1, 0).start()
        if k in DIRECT:
            l2c(k, e, 0).start()

    def l_fwd(k, *es):
        for e in es:
            def go(e=e):
                i, who = (0, 3) if e < 2 else (1, 1)
                pc(k, e, i, who).wait_recv()
                if k not in DIRECT:
                    qc(k, e, who).start()
            on(k, e, go)

    def l_other(k):
        for e in range(4):
            def go(e=e):
                i, who = (1, 1) if e < 2 else (0, 3)
                pc(k, e, i, who).wait_recv()
            on(k, e, go)

    def l_last(k):
        for e in range(4):
            on(k, e, lambda e=e: (l2c if k in DIRECT else qc)(k, e, 2).wait_recv())

    def s_send(k, *ws):
        for w in ws:
            sc(k, w, core).start()

    def s_wait(k):
        blk = wall.at[1 - core, zof[k]]
        copy(blk, blk, w_s, c_r.at[k], sib).wait_recv()

    zc(0).start()
    zc(1).start()

    @pl.when(first)
    def _():
        f_send(0)

    @pl.when(jnp.logical_not(first))
    def _():
        for e in (0, 1, 3, 2):
            l_send(0, e)

    zc(2).start()

    old = lax.broadcasted_iota(jnp.int32, (CH, 128), 0)
    shift_by = jnp.zeros((CH, 128), jnp.int32)
    for i in range(16):
        d = (i % 4 - zh + 4) % 4
        k = jnp.where(d == 0, 0, jnp.where(d == 3, 1, jnp.where(d == 1, 2, 3)))
        j = k * 4 + i // 4
        shift_by = jnp.where(old >= 40 * i, 40 * (j - i), shift_by)
    target = old + shift_by
    lane0 = lax.broadcasted_iota(jnp.int32, (CH, 128), 1)
    perm = jnp.concatenate(
        [jnp.where(target == lane0 + 128 * n, 1.0, 0.0).astype(BF) for n in range(5)], axis=1
    )

    feat_in.wait()

    def stage(p, _):
        r = 2 * p
        two = jnp.concatenate([feat_raw[r].astype(F32), feat_raw[r + 1].astype(F32)], axis=0)
        feat[p] = two.astype(BF)
        return 0

    lax.fori_loop(0, R // 2, stage, 0)
    def reorder(h, _):
        v = dot(feat[pl.ds(5 * h, 5)].reshape(400, CH), perm)
        acc[pl.ds(pl.multiple_of(400 * h, 400), 400), :] = v
        return 0

    lax.fori_loop(0, 2, reorder, 0)

    @pl.when(first)
    def _():
        f_fwd(0)
        l_send(0, 1)
        l_send(0, 3)

    l_fwd(0, 0)

    def pass1(p, total):
        r = 2 * p
        v = acc[pl.ds(pl.multiple_of(80 * p, 80), 80), :]
        feat[p] = v.astype(BF)
        col_out[0, pl.ds(r, 1), :] = v[0:1]
        col_out[1, pl.ds(r, 1), :] = v[39:40]
        col_out[0, pl.ds(r + 1, 1), :] = v[40:41]
        col_out[1, pl.ds(r + 1, 1), :] = v[79:80]
        for i in range(10):
            total = total + v[8 * i : 8 * i + 8]
        return total

    zeros = jnp.zeros((8, CH), F32)
    col_out[0, 16:24, :] = zeros
    col_out[1, 16:24, :] = zeros
    total = lax.fori_loop(0, R // 2, pass1, zeros)

    @pl.when(first)
    def _():
        f_done(0)
        l_send(0, 2)

    s_send(0, 0)


    halo = [
        (feat.at[R // 2 - 1], row_in.at[0], (dp, down, col)),
        (feat.at[0], row_in.at[1], (dp, up, col)),
        (col_out.at[1], col_in.at[0], (dp, row, right)),
        (col_out.at[0], col_in.at[1], (dp, row, left)),
        (col_out.at[1, pl.ds(16, 8)], cor_in.at[0], (dp, down, right)),
        (col_out.at[0, pl.ds(16, 8)], cor_in.at[1], (dp, down, left)),
        (col_out.at[1, pl.ds(0, 8)], cor_in.at[2], (dp, up, right)),
        (col_out.at[0, pl.ds(0, 8)], cor_in.at[3], (dp, up, left)),
    ]
    around = [
        (dp, down, right), (dp, down, col), (dp, down, left),
        (dp, row, right), (dp, row, left),
        (dp, up, right), (dp, up, col), (dp, up, left),
    ]
    halo += [(mask, mask_in.at[i], d) for i, d in enumerate(around)]
    hcs = [
        copy(s, d, h_s.at[i], h_r.at[i] if i < 8 else m_r, dev)
        for i, (s, d, dev) in enumerate(halo)
    ]
    for c in hcs:
        c.start()

    chan = lax.broadcasted_iota(jnp.int32, (CH, 128), 0)
    lane = lax.broadcasted_iota(jnp.int32, (CH, 128), 1)
    per = CH // GROUPS
    gm = jnp.where((chan >= lane * per) & (chan < lane * per + per), 1.0, 0.0).astype(BF)
    gm = lax.dot_general(perm, gm, (((0,), (0,)), ((), ())), preferred_element_type=F32).astype(BF)
    lane_t = lax.broadcasted_iota(jnp.int32, (128, CH), 0)
    chan_t = lax.broadcasted_iota(jnp.int32, (128, CH), 1)
    gt = jnp.where((chan_t >= lane_t * per) & (chan_t < lane_t * per + per), 1.0, 0.0).astype(BF)
    gt = dot(gt, perm).astype(BF)

    def spread(v):
        return jnp.broadcast_to(jnp.sum(v, axis=0, keepdims=True), v.shape)

    n_here = float(R * C * per)
    mean_here = dot3(spread(total), gm) * (1.0 / n_here)
    mean_chan = dot3(mean_here, gt)[0:1]

    def pass2(p, total):
        d = feat[p].astype(F32) - mean_chan
        d = d * d
        for i in range(10):
            total = total + d[8 * i : 8 * i + 8]
        return total

    m2 = dot3(spread(lax.fori_loop(0, R // 2, pass2, zeros)), gm)
    sub = lax.broadcasted_iota(jnp.int32, (8, 128), 0)
    st_out[...] = jnp.where(sub == 0, mean_here, m2)

    def tc(t):
        return copy(st_out, st_in.at[t], t_s, t_r, peer(t))

    def st_send(t, _):
        tc(t).start()
        return 0

    lax.fori_loop(1, 32, st_send, 0)

    zin(1).wait_recv()
    l_send(1, 0)
    f_send(1)
    zin(2).wait_recv()
    l_send(2, 0)
    f_send(2)
    l_fwd(0, 1, 3)

    copy(mask_in, mask_in, h_s.at[0], m_r, sib).wait_recv()

    lane1 = lax.broadcasted_iota(jnp.int32, (R, 128), 1)

    def wide(v):
        return jnp.concatenate([v.astype(F32), jnp.zeros((R, 128 - C), F32)], axis=1)

    def strip(lef, mid, rig):
        a = pltpu.roll(wide(lef), 128 - 39, 1)
        b = pltpu.roll(wide(mid), 1, 1)
        c = pltpu.roll(wide(rig), 41, 1)
        res = jnp.where((lane1 >= 1) & (lane1 <= 40), b, 0.0)
        res = jnp.where((lane1 == 0) & (col > 0), a, res)
        return jnp.where((lane1 == 41) & (col < 3), c, res)

    above = strip(mask_in[0], mask_in[1], mask_in[2])
    here = strip(mask_in[3], mask[...], mask_in[4])
    below = strip(mask_in[5], mask_in[6], mask_in[7])
    mpad[...] = jnp.zeros((128, 128), F32)
    mpad[0:1, :] = jnp.where(row > 0, above[19:20], 0.0)
    mpad[1:21, :] = here
    mpad[21:22, :] = jnp.where(row < 7, below[0:1], 0.0)
    mcols[...] = mpad[...].T
    d3 = mcols[0:40, :] + pltpu.roll(mcols[1:41, :], 32, 1) + pltpu.roll(mcols[2:42, :], 64, 1)

    def fill_mask(p, _):
        a = pltpu.roll(d3, lax.rem(128 - 2 * p, 128), 1)
        b = pltpu.roll(d3, lax.rem(127 - 2 * p, 128), 1)
        mtaps[pl.ds(pl.multiple_of(80 * p, 80), 80), :] = jnp.concatenate([a, b], axis=0).astype(BF)
        return 0

    lax.fori_loop(0, 10, fill_mask, 0)
    gtab[...] = jnp.zeros((128, CH), F32)
    for dy in range(3):
        for dx in range(3):
            gtab[32 * dx + dy : 32 * dx + dy + 1, :] = mask_w[3 * dy + dx : 3 * dy + dx + 1, :]
    g = gtab[...]
    g_hi = g.astype(BF)
    g_rest = g - g_hi.astype(F32)
    g_mid = g_rest.astype(BF)
    g_low = (g_rest - g_mid.astype(F32)).astype(BF)
    bias_row = bias[...].reshape(1, CH)

    g_all = jnp.concatenate([g_hi, g_mid, g_low], axis=0)

    def mask_term(h, _):
        rows = pl.ds(pl.multiple_of(400 * h, 400), 400)
        m = mtaps[rows, :]
        acc[rows, :] = dot(jnp.concatenate([m, m, m], axis=1), g_all) + bias_row
        return 0

    lax.fori_loop(0, 2, mask_term, 0)

    f_fwd(1)
    l_send(1, 1)
    l_send(1, 3)
    f_fwd(2)
    l_send(2, 1)
    l_send(2, 3)
    l_fwd(0, 2)

    copy(st_in.at[pl.ds(1, 31)], st_in.at[pl.ds(1, 31)], t_s, t_r, sib).wait_recv()

    def st_mean(t, total):
        return total + st_in[t]

    mean_g = lax.fori_loop(1, 32, st_mean, st_out[...])[0:1] * (1.0 / 32.0)

    def st_sq(t, total):
        v = st_in[t]
        dm = v[0:1] - mean_g
        return total + v[1:2] + n_here * dm * dm

    dm = st_out[0:1, :] - mean_g
    sq = lax.fori_loop(1, 32, st_sq, st_out[1:2, :] + n_here * dm * dm)
    rs_g = lax.rsqrt(sq * (1.0 / (32.0 * n_here)) + EPS)
    both_g = dot3(jnp.concatenate([mean_g, rs_g, jnp.zeros((6, 128), F32)], axis=0), gt)
    mean_c, rs_c = both_g[0:1], both_g[1:2]
    gs = jnp.concatenate(
        [gain[...].reshape(1, CH), shift[...].reshape(1, CH), jnp.zeros((6, CH), F32)], axis=0
    )
    gs = dot3(gs, perm)
    gain_c, shift_c = gs[0:1], gs[1:2]

    def activate(v):
        v = (v - mean_c) * rs_c * gain_c + shift_c
        return v / (1.0 + jnp.exp(-v))

    def act_rows(p, _):
        v = activate(feat[p].astype(F32))
        act[2 * p + 1, 8 : 8 + C, :] = v[0:C]
        act[2 * p + 2, 8 : 8 + C, :] = v[C : 2 * C]
        return 0

    f_done(1)
    l_send(1, 2)
    f_done(2)
    l_send(2, 2)
    lax.fori_loop(0, 5, act_rows, 0)
    zin(3).wait_recv()
    l_send(3, 0)
    f_send(3)
    s_send(1, 0)
    s_send(2, 0)
    l_other(0)
    s_send(0, 1, 3)
    lax.fori_loop(5, 10, act_rows, 0)
    f_fwd(3)
    l_send(3, 1)
    l_send(3, 3)
    l_last(0)
    s_send(0, 2)

    for c in hcs[:8]:
        c.wait_recv()
    act[0, 8 : 8 + C, :] = jnp.where(row > 0, activate(row_in[0].astype(F32)[40:80]), 0.0)
    act[21, 8 : 8 + C, :] = jnp.where(row < 7, activate(row_in[1].astype(F32)[0:40]), 0.0)
    for side, there, off in ((0, col > 0, 7), (1, col < 3, 48)):
        edge = jnp.where(there, activate(col_in[side]), 0.0)
        for r in range(R):
            act[r + 1, off : off + 1, :] = edge[r : r + 1]
    for i, (there, pick, r, spot) in enumerate((
        ((row > 0) & (col > 0), 3, 0, 7),
        ((row > 0) & (col < 3), 3, 0, 48),
        ((row < 7) & (col > 0), 0, 21, 7),
        ((row < 7) & (col < 3), 0, 21, 48),
    )):
        corner = jnp.where(there, activate(cor_in[i]), 0.0)
        act[r, spot : spot + 1, :] = corner[pick : pick + 1]

    f_done(3)
    l_send(3, 2)
    s_send(3, 0)

    def fill(p, _):
            r = jnp.where(p < 11, 2 * p, 2 * p - 21)
            for dx in range(3):
                a = act[r, 7 + dx : 7 + dx + C, :]
                b = act[r + 1, 7 + dx : 7 + dx + C, :]
                v = jnp.concatenate([a, b], axis=0).astype(BF)
                taps[dx, pl.ds(pl.multiple_of(80 * p, 80), 80), :] = v
            return 0

    lax.fori_loop(0, 21, fill, 0)

    low_half = lax.broadcasted_iota(jnp.int32, (16, 128), 0) < 8

    def delta(k):
        return jnp.where(k == 0, 0, jnp.where(k == 1, 3, jnp.where(k == 2, 1, 2)))

    def merge(k, _):
        z = lax.rem(zh + delta(k), 4)

        for m in range(2):
            base = pl.multiple_of(jnp.where(k == 0, 0, 128 + 160 * k) + 80 * m, 16)
            rows = pl.ds(base, 80)
            ya, yb = 2 * m, 2 * m + 1

            def two(j, _):
                for n in range(5):
                    if n < 3:
                        a = wall.at[0, z, j, ya, pl.ds(80 * n, 80)]
                        b = wall.at[0, z, j, yb, pl.ds(80 * n, 80)]
                    else:
                        a = wall.at[1, z, ya, j, pl.ds(80 * (n - 3), 80)]
                        b = wall.at[1, z, yb, j, pl.ds(80 * (n - 3), 80)]
                    a2, b2 = a[32:48, :].astype(F32), b[32:48, :].astype(F32)
                    mid_s = jnp.where(low_half, a2, b2).astype(BF)
                    mid_t = jnp.concatenate([a2[8:16], b2[0:8]], axis=0).astype(BF)
                    ln = pl.ds(128 * n, 128)
                    wm[2 * j, rows, ln] = jnp.concatenate(
                        [a[0:32, :], mid_s, b[0:32, :]], axis=0
                    )
                    wm[2 * j + 1, rows, ln] = jnp.concatenate(
                        [a[48:80, :], mid_t, b[48:80, :]], axis=0
                    )
                return 0

            lax.fori_loop(0, 4, two, 0)

            def tile(y_, n, r):
                i = 3 * n + r
                return wall[1, z, y_, i // 4, pl.ds(160 + 16 * (i % 4), 16), :]

            for n in range(5):
                mid = jnp.where(low_half, tile(ya, n, 2).astype(F32), tile(yb, n, 0).astype(F32))
                wm[8, rows, pl.ds(128 * n, 128)] = jnp.concatenate(
                    [tile(ya, n, 0), tile(ya, n, 1), mid.astype(BF), tile(yb, n, 1), tile(yb, n, 2)],
                    axis=0,
                )
        return 0

    def conv(w, dy):
        lane_at = jnp.where(w == 0, 0, jnp.where(w == 1, 128, 384))
        win = pl.ds(pl.multiple_of(lane_at, 128), 256)
        start = pl.multiple_of(jnp.where(dy == 0, 0, jnp.where(dy == 1, 880, 80)), 80)
        parts = [taps[dx, pl.ds(start, R * C), win] for dx in range(3)]
        rhs = wm[pl.ds(3 * dy, 3), pl.ds(pl.multiple_of(256 * w, 256), 256), :].reshape(768, CH)
        acc[...] += dot(jnp.concatenate(parts, axis=1), rhs)

    def arrive(k):
        l_fwd(k, 0, 1, 3, 2)
        l_other(k)
        s_send(k, 1, 3)
        l_last(k)
        s_send(k, 2)

    def step(t, _):
        w, dy = t // 3, lax.rem(t, 3)

        def when(there, *fs):
            @pl.when(t == there)
            def _():
                for f in fs:
                    f()

        when(0, lambda: s_wait(0))
        when(1, lambda: arrive(1))
        when(2, lambda: arrive(2))
        when(3, lambda: s_wait(1), lambda: s_wait(2))
        when(4, lambda: arrive(3))
        when(6, lambda: s_wait(3))

        @pl.when(dy == 0)
        def _():
            lo = jnp.where(w == 0, 0, jnp.where(w == 1, 1, 3))
            hi = jnp.where(w == 0, 1, jnp.where(w == 1, 3, 4))
            lax.fori_loop(lo, hi, merge, 0)

        conv(w, dy)
        return 0

    lax.fori_loop(0, 9, step, 0)

    def finish(r, _):
        out4[0, r] = acc[pl.ds(pl.multiple_of(C * r, 8), C), :].astype(BF)
        return 0

    lax.fori_loop(0, R, finish, 0)

    for blk in (wall.at[0], wall.at[1, pl.ds(0, 3)], wall.at[1, 3, pl.ds(0, 3)]):
        copy(blk, blk, w_s, z_r.at[0], sib).wait_send()
    for c in hcs:
        c.wait_send()
    copy(st_in.at[pl.ds(1, 31)], st_in.at[pl.ds(1, 31)], t_s, t_r, sib).wait_send()


def local(features, hole_mask, norm_gain, norm_shift, conv_weight, mask_weight, conv_bias):
    vm = pl.BlockSpec(memory_space=pltpu.VMEM)
    dma = pltpu.SemaphoreType.DMA
    result = pl.pallas_call(
        kernel,
        out_shape=jax.ShapeDtypeStruct((1, R, C, CH), BF),
        in_specs=[pl.BlockSpec(memory_space=pl.ANY)] + [vm] * 6,
        out_specs=vm,
        scratch_shapes=[
            pltpu.VMEM((2, 4, 4, 4, BLK, 128), BF),
            pltpu.VMEM((9, 768, CH), BF),
            pltpu.VMEM((22, STRIDE, CH), F32),
            pltpu.VMEM((3, 42 * C, CH), BF),
            pltpu.VMEM((R * C, CH), F32),
            pltpu.VMEM((R, C), jnp.int32),
            pltpu.VMEM((R // 2, 2 * C, CH), BF),
            pltpu.VMEM((2, 24, CH), F32),
            pltpu.VMEM((2, 2 * C, CH), BF),
            pltpu.VMEM((2, 24, CH), F32),
            pltpu.VMEM((4, 8, CH), F32),
            pltpu.VMEM((8, R, C), jnp.int32),
            pltpu.VMEM((128, 128), F32),
            pltpu.VMEM((128, 128), F32),
            pltpu.VMEM((R * C, 128), BF),
            pltpu.VMEM((128, CH), F32),
            pltpu.VMEM((8, 128), F32),
            pltpu.VMEM((32, 8, 128), F32),
            dma(()), dma((3,)), dma((4, 2)), dma((4, 2)), dma((4, 4, 2)), dma((4, 4)), dma((4,)),
            dma((16,)), dma((8,)), dma(()), dma(()), dma(()), dma(()),
            pltpu.VMEM((R, C, CH), BF),
        ],
        compiler_params=pltpu.CompilerParams(
            collective_id=0, has_side_effects=True, vmem_limit_bytes=56 << 20
        ),
        name="conv",
    )(features, hole_mask.reshape(R, 1, C), norm_gain, norm_shift, conv_weight, mask_weight, conv_bias)
    return result


def solution(mesh):
    image = P("dp", "row", "col", None)
    return jax.shard_map(
        local,
        mesh=mesh,
        in_specs=(image, P("dp", "row", "col"), P(), P(), P(None, "dp", None), P(), P()),
        out_specs=image,
        check_vma=False,
    )
```

```python
import jax
import jax.numpy as jnp
from jax import lax
from jax.experimental import pallas as pl
from jax.experimental.pallas import tpu as pltpu
from jax.sharding import PartitionSpec as P

GROUPS = 32
EPS = 1e-05
MESH = pl.DeviceIdType.MESH
BF = jnp.bfloat16
F32 = jnp.float32
R, C, CH = 20, 40, 640
BLK = 240
CUT = 128
STRIDE = 56
DELTAS = (0, 3, 1, 2)
DIRECT = (1, 2, 3)


def dot(a, b):
    return jnp.dot(a, b, preferred_element_type=F32)


def dot3(a, b):
    hi = a.astype(BF)
    rest = a - hi.astype(F32)
    mid = rest.astype(BF)
    low = (rest - mid.astype(F32)).astype(BF)
    return dot(hi, b) + dot(mid, b) + dot(low, b)


def kernel(
    feat4, mask3, gain, shift, weight, mask_w, bias, out4,
    wall, wm, act, taps, acc, mask, feat, col_out, row_in, col_in, cor_in,
    mask_in, mpad, mcols, mtaps, gtab, st_out, st_in,
    w_s, z_r, f_r, fh_r, p_r, q_r, c_r, h_s, h_r, m_r, t_s, t_r, in_sem, feat_raw,
):
    dp, row, col = lax.axis_index("dp"), lax.axis_index("row"), lax.axis_index("col")
    x, core = row // 2, row % 2
    y, zh = dp // 4, dp % 4

    def at(y_, zh_, x_, core_, col_):
        return (y_ * 4 + zh_, x_ * 2 + core_, col_)

    up, down = (row + 7) % 8, (row + 1) % 8
    left, right = (col + 3) % 4, (col + 1) % 4
    far = [at(y, (zh + s) % 4, x, core, col) for s in (1, 3, 2)]
    xn = [at(y, zh, (x + 1) % 4, core, col), at(y, zh, (x + 3) % 4, core, col)]
    yn = [at((y + 1) % 4, zh, x, core, col), at((y + 3) % 4, zh, x, core, col)]
    first = core == 0
    fdev = [tuple(jnp.where(first, a, b) for a, b in zip(yn[i], xn[i])) for i in range(2)]
    ldev = [tuple(jnp.where(first, b, a) for a, b in zip(yn[i], xn[i])) for i in range(2)]
    sib = at(y, zh, x, 1 - core, col)
    fme = jnp.where(first, y, x)
    lme = jnp.where(first, x, y)
    zof = [(zh + d) % 4 for d in DELTAS]

    feat_in = pltpu.make_async_copy(feat4.at[0], feat_raw, in_sem)
    feat_in.start()
    barrier = pltpu.get_barrier_semaphore()
    x2, y2 = at(y, zh, (x + 2) % 4, core, col), at((y + 2) % 4, zh, x, core, col)
    f2 = tuple(jnp.where(first, a, b) for a, b in zip(y2, x2))
    l2 = tuple(jnp.where(first, b, a) for a, b in zip(y2, x2))
    for d in far + yn + [y2]:
        pl.semaphore_signal(barrier, inc=1, device_id=d, device_id_type=MESH)

    def peer(t):
        return (dp, (row + t // 4) % 8, (col + t % 4) % 4)

    def greet(t, _):
        pl.semaphore_signal(barrier, inc=1, device_id=peer(t), device_id_type=MESH)
        return 0

    lax.fori_loop(1, 32, greet, 0)

    for r in range(R):
        mask[r : r + 1, :] = mask3[r]

    isodd = y % 2 == 1
    zero8 = jnp.zeros((8, CH), F32)

    def both(a, b):
        return jnp.where(isodd, b, a)

    def pair(j):
        s, t = weight[2 * j].astype(F32), weight[2 * j + 1].astype(F32)
        a = jnp.concatenate([s, t[32:40], t[0:32]], axis=0)
        b = jnp.concatenate([s[8:40], t[0:8], s[0:8], t[8:40]], axis=0)
        return both(a, b).astype(BF)

    @pl.when(first)
    def _():
        for j in range(4):
            v = pair(j)
            for n in range(3):
                wall[0, zh, j, y, 80 * n : 80 * n + 80, :] = v[:, 128 * n : 128 * n + 128]

    @pl.when(jnp.logical_not(first))
    def _():
        last = weight[8].astype(F32)
        tail = both(
            jnp.concatenate([last, zero8], axis=0), jnp.concatenate([zero8, last], axis=0)
        ).astype(BF)
        for j in range(4):
            v = pair(j)
            for n in range(2):
                wall[1, zh, y, j, 80 * n : 80 * n + 80, :] = v[:, 384 + 128 * n : 512 + 128 * n]
            for s in range(4):
                m = 4 * j + s
                if m < 15:
                    n, r = m // 3, m % 3
                    wall[1, zh, y, j, 160 + 16 * s : 176 + 16 * s, :] = tail[
                        16 * r : 16 * r + 16, 128 * n : 128 * n + 128
                    ]
                else:
                    wall[1, zh, y, j, 160 + 16 * s : 176 + 16 * s, :] = jnp.zeros((16, 128), BF)
            wall[1, zh, y, j, 224:240, :] = jnp.zeros((16, 128), BF)

    def clear(t, _):
        wm[t, 160:288] = jnp.zeros((128, CH), BF)
        return 0

    lax.fori_loop(0, 9, clear, 0)
    pl.semaphore_wait(barrier, 37)

    def copy(src, dst, s, r, d):
        return pltpu.make_async_remote_copy(src, dst, s, r, device_id=d, device_id_type=MESH)

    def zc(i):
        blk = wall.at[core, zh, lme, fme]
        return copy(blk, blk, w_s, z_r.at[i], far[i])

    def zin(k):
        i = {3: 0, 1: 1, 2: 2}[DELTAS[k]]
        blk = wall.at[core, zof[k], lme, fme]
        return copy(blk, blk, w_s, z_r.at[i], far[i])

    def fc(k, i, who):
        blk = wall.at[core, zof[k], lme, (fme + who) % 4]
        return copy(blk, blk, w_s, f_r.at[k, i], fdev[i])

    def fhc(k, i, who):
        rows = pl.ds(0, CUT) if i == 0 else pl.ds(CUT, BLK - CUT)
        blk = wall.at[core, zof[k], lme, (fme + who) % 4, rows]
        return copy(blk, blk, w_s, fh_r.at[k, i], fdev[i])

    def pc(k, e, i, who):
        blk = wall.at[core, zof[k], (lme + who) % 4, (fme + e) % 4]
        return copy(blk, blk, w_s, p_r.at[k, e, i], ldev[i])

    def qc(k, e, who):
        blk = wall.at[core, zof[k], (lme + who) % 4, (fme + e) % 4]
        return copy(blk, blk, w_s, q_r.at[k, e], ldev[0 if e < 2 else 1])

    def sc(k, w, which):
        l_there = jnp.where(core == which, lme, jnp.where(first, y, x))
        blk = wall.at[which, zof[k], (l_there + w) % 4]
        return copy(blk, blk, w_s, c_r.at[k], sib)

    def f2c(k, who):
        blk = wall.at[core, zof[k], lme, (fme + who) % 4]
        return copy(blk, blk, w_s, fh_r.at[k, 0], f2)

    def l2c(k, e, who):
        blk = wall.at[core, zof[k], (lme + who) % 4, (fme + e) % 4]
        return copy(blk, blk, w_s, q_r.at[k, e], l2)

    def f_send(k):
        fc(k, 0, 0).start()
        fc(k, 1, 0).start()
        if k in DIRECT:
            f2c(k, 0).start()

    def f_fwd(k):
        fc(k, 0, 3).wait_recv()
        if k not in DIRECT:
            fhc(k, 0, 3).start()
        fc(k, 1, 1).wait_recv()
        if k not in DIRECT:
            fhc(k, 1, 1).start()

    def f_done(k):
        if k in DIRECT:
            f2c(k, 2).wait_recv()
        else:
            fhc(k, 0, 2).wait_recv()
            fhc(k, 1, 2).wait_recv()

    def on(k, e, cond_fn):
        if k == 0 and e == 0:
            pl.when(jnp.logical_not(first))(cond_fn)
        else:
            cond_fn()

    def l_send(k, e):
        pc(k, e, 0, 0).start()
        pc(k, e, 1, 0).start()
        if k in DIRECT:
            l2c(k, e, 0).start()

    def l_fwd(k, *es):
        for e in es:
            def go(e=e):
                i, who = (0, 3) if e < 2 else (1, 1)
                pc(k, e, i, who).wait_recv()
                if k not in DIRECT:
                    qc(k, e, who).start()
            on(k, e, go)

    def l_other(k):
        for e in range(4):
            def go(e=e):
                i, who = (1, 1) if e < 2 else (0, 3)
                pc(k, e, i, who).wait_recv()
            on(k, e, go)

    def l_last(k):
        for e in range(4):
            on(k, e, lambda e=e: (l2c if k in DIRECT else qc)(k, e, 2).wait_recv())

    def s_send(k, *ws):
        for w in ws:
            sc(k, w, core).start()

    def s_wait(k):
        blk = wall.at[1 - core, zof[k]]
        copy(blk, blk, w_s, c_r.at[k], sib).wait_recv()

    zc(0).start()
    zc(1).start()

    @pl.when(first)
    def _():
        f_send(0)

    @pl.when(jnp.logical_not(first))
    def _():
        for e in (0, 1, 3, 2):
            l_send(0, e)

    zc(2).start()

    old = lax.broadcasted_iota(jnp.int32, (CH, 128), 0)
    shift_by = jnp.zeros((CH, 128), jnp.int32)
    for i in range(16):
        d = (i % 4 - zh + 4) % 4
        k = jnp.where(d == 0, 0, jnp.where(d == 3, 1, jnp.where(d == 1, 2, 3)))
        j = k * 4 + i // 4
        shift_by = jnp.where(old >= 40 * i, 40 * (j - i), shift_by)
    target = old + shift_by
    lane0 = lax.broadcasted_iota(jnp.int32, (CH, 128), 1)
    perm = jnp.concatenate(
        [jnp.where(target == lane0 + 128 * n, 1.0, 0.0).astype(BF) for n in range(5)], axis=1
    )

    feat_in.wait()

    def stage(p, _):
        r = 2 * p
        two = jnp.concatenate([feat_raw[r].astype(F32), feat_raw[r + 1].astype(F32)], axis=0)
        feat[p] = two.astype(BF)
        return 0

    lax.fori_loop(0, R // 2, stage, 0)
    def reorder(h, _):
        v = dot(feat[pl.ds(5 * h, 5)].reshape(400, CH), perm)
        acc[pl.ds(pl.multiple_of(400 * h, 400), 400), :] = v
        return 0

    lax.fori_loop(0, 2, reorder, 0)

    @pl.when(first)
    def _():
        f_fwd(0)
        l_send(0, 1)
        l_send(0, 3)

    l_fwd(0, 0)

    def pass1(p, total):
        r = 2 * p
        v = acc[pl.ds(pl.multiple_of(80 * p, 80), 80), :]
        feat[p] = v.astype(BF)
        col_out[0, pl.ds(r, 1), :] = v[0:1]
        col_out[1, pl.ds(r, 1), :] = v[39:40]
        col_out[0, pl.ds(r + 1, 1), :] = v[40:41]
        col_out[1, pl.ds(r + 1, 1), :] = v[79:80]
        for i in range(10):
            total = total + v[8 * i : 8 * i + 8]
        return total

    zeros = jnp.zeros((8, CH), F32)
    col_out[0, 16:24, :] = zeros
    col_out[1, 16:24, :] = zeros
    total = lax.fori_loop(0, R // 2, pass1, zeros)

    @pl.when(first)
    def _():
        f_done(0)
        l_send(0, 2)

    s_send(0, 0)


    halo = [
        (feat.at[R // 2 - 1], row_in.at[0], (dp, down, col)),
        (feat.at[0], row_in.at[1], (dp, up, col)),
        (col_out.at[1], col_in.at[0], (dp, row, right)),
        (col_out.at[0], col_in.at[1], (dp, row, left)),
        (col_out.at[1, pl.ds(16, 8)], cor_in.at[0], (dp, down, right)),
        (col_out.at[0, pl.ds(16, 8)], cor_in.at[1], (dp, down, left)),
        (col_out.at[1, pl.ds(0, 8)], cor_in.at[2], (dp, up, right)),
        (col_out.at[0, pl.ds(0, 8)], cor_in.at[3], (dp, up, left)),
    ]
    around = [
        (dp, down, right), (dp, down, col), (dp, down, left),
        (dp, row, right), (dp, row, left),
        (dp, up, right), (dp, up, col), (dp, up, left),
    ]
    halo += [(mask, mask_in.at[i], d) for i, d in enumerate(around)]
    hcs = [
        copy(s, d, h_s.at[i], h_r.at[i] if i < 8 else m_r, dev)
        for i, (s, d, dev) in enumerate(halo)
    ]
    for c in hcs:
        c.start()

    chan = lax.broadcasted_iota(jnp.int32, (CH, 128), 0)
    lane = lax.broadcasted_iota(jnp.int32, (CH, 128), 1)
    per = CH // GROUPS
    gm = jnp.where((chan >= lane * per) & (chan < lane * per + per), 1.0, 0.0).astype(BF)
    gm = lax.dot_general(perm, gm, (((0,), (0,)), ((), ())), preferred_element_type=F32).astype(BF)
    lane_t = lax.broadcasted_iota(jnp.int32, (128, CH), 0)
    chan_t = lax.broadcasted_iota(jnp.int32, (128, CH), 1)
    gt = jnp.where((chan_t >= lane_t * per) & (chan_t < lane_t * per + per), 1.0, 0.0).astype(BF)
    gt = dot(gt, perm).astype(BF)

    def spread(v):
        return jnp.broadcast_to(jnp.sum(v, axis=0, keepdims=True), v.shape)

    n_here = float(R * C * per)
    mean_here = dot3(spread(total), gm) * (1.0 / n_here)
    mean_chan = dot3(mean_here, gt)[0:1]

    def pass2(p, total):
        d = feat[p].astype(F32) - mean_chan
        d = d * d
        for i in range(10):
            total = total + d[8 * i : 8 * i + 8]
        return total

    m2 = dot3(spread(lax.fori_loop(0, R // 2, pass2, zeros)), gm)
    sub = lax.broadcasted_iota(jnp.int32, (8, 128), 0)
    st_out[...] = jnp.where(sub == 0, mean_here, m2)

    def tc(t):
        return copy(st_out, st_in.at[t], t_s, t_r, peer(t))

    def st_send(t, _):
        tc(t).start()
        return 0

    lax.fori_loop(1, 32, st_send, 0)

    zin(1).wait_recv()
    l_send(1, 0)
    f_send(1)
    zin(2).wait_recv()
    l_send(2, 0)
    f_send(2)
    l_fwd(0, 1, 3)

    copy(mask_in, mask_in, h_s.at[0], m_r, sib).wait_recv()

    lane1 = lax.broadcasted_iota(jnp.int32, (R, 128), 1)

    def wide(v):
        return jnp.concatenate([v.astype(F32), jnp.zeros((R, 128 - C), F32)], axis=1)

    def strip(lef, mid, rig):
        a = pltpu.roll(wide(lef), 128 - 39, 1)
        b = pltpu.roll(wide(mid), 1, 1)
        c = pltpu.roll(wide(rig), 41, 1)
        res = jnp.where((lane1 >= 1) & (lane1 <= 40), b, 0.0)
        res = jnp.where((lane1 == 0) & (col > 0), a, res)
        return jnp.where((lane1 == 41) & (col < 3), c, res)

    above = strip(mask_in[0], mask_in[1], mask_in[2])
    here = strip(mask_in[3], mask[...], mask_in[4])
    below = strip(mask_in[5], mask_in[6], mask_in[7])
    mpad[...] = jnp.zeros((128, 128), F32)
    mpad[0:1, :] = jnp.where(row > 0, above[19:20], 0.0)
    mpad[1:21, :] = here
    mpad[21:22, :] = jnp.where(row < 7, below[0:1], 0.0)
    mcols[...] = mpad[...].T
    d3 = mcols[0:40, :] + pltpu.roll(mcols[1:41, :], 32, 1) + pltpu.roll(mcols[2:42, :], 64, 1)

    def fill_mask(p, _):
        a = pltpu.roll(d3, lax.rem(128 - 2 * p, 128), 1)
        b = pltpu.roll(d3, lax.rem(127 - 2 * p, 128), 1)
        mtaps[pl.ds(pl.multiple_of(80 * p, 80), 80), :] = jnp.concatenate([a, b], axis=0).astype(BF)
        return 0

    lax.fori_loop(0, 10, fill_mask, 0)
    gtab[...] = jnp.zeros((128, CH), F32)
    for dy in range(3):
        for dx in range(3):
            gtab[32 * dx + dy : 32 * dx + dy + 1, :] = mask_w[3 * dy + dx : 3 * dy + dx + 1, :]
    g = gtab[...]
    g_hi = g.astype(BF)
    g_rest = g - g_hi.astype(F32)
    g_mid = g_rest.astype(BF)
    g_low = (g_rest - g_mid.astype(F32)).astype(BF)
    bias_row = bias[...].reshape(1, CH)

    g_all = jnp.concatenate([g_hi, g_mid, g_low], axis=0)

    def mask_term(h, _):
        rows = pl.ds(pl.multiple_of(400 * h, 400), 400)
        m = mtaps[rows, :]
        acc[rows, :] = dot(jnp.concatenate([m, m, m], axis=1), g_all) + bias_row
        return 0

    lax.fori_loop(0, 2, mask_term, 0)

    f_fwd(1)
    l_send(1, 1)
    l_send(1, 3)
    f_fwd(2)
    l_send(2, 1)
    l_send(2, 3)
    l_fwd(0, 2)

    copy(st_in.at[pl.ds(1, 31)], st_in.at[pl.ds(1, 31)], t_s, t_r, sib).wait_recv()

    def st_mean(t, total):
        return total + st_in[t]

    mean_g = lax.fori_loop(1, 32, st_mean, st_out[...])[0:1] * (1.0 / 32.0)

    def st_sq(t, total):
        v = st_in[t]
        dm = v[0:1] - mean_g
        return total + v[1:2] + n_here * dm * dm

    dm = st_out[0:1, :] - mean_g
    sq = lax.fori_loop(1, 32, st_sq, st_out[1:2, :] + n_here * dm * dm)
    rs_g = lax.rsqrt(sq * (1.0 / (32.0 * n_here)) + EPS)
    both_g = dot3(jnp.concatenate([mean_g, rs_g, jnp.zeros((6, 128), F32)], axis=0), gt)
    mean_c, rs_c = both_g[0:1], both_g[1:2]
    gs = jnp.concatenate(
        [gain[...].reshape(1, CH), shift[...].reshape(1, CH), jnp.zeros((6, CH), F32)], axis=0
    )
    gs = dot3(gs, perm)
    gain_c, shift_c = gs[0:1], gs[1:2]

    def activate(v):
        v = (v - mean_c) * rs_c * gain_c + shift_c
        return v / (1.0 + jnp.exp(-v))

    def act_rows(p, _):
        v = activate(feat[p].astype(F32))
        act[2 * p + 1, 8 : 8 + C, :] = v[0:C]
        act[2 * p + 2, 8 : 8 + C, :] = v[C : 2 * C]
        return 0

    f_done(1)
    l_send(1, 2)
    f_done(2)
    l_send(2, 2)
    lax.fori_loop(0, 5, act_rows, 0)
    zin(3).wait_recv()
    l_send(3, 0)
    f_send(3)
    s_send(1, 0)
    s_send(2, 0)
    l_other(0)
    s_send(0, 1, 3)
    lax.fori_loop(5, 10, act_rows, 0)
    f_fwd(3)
    l_send(3, 1)
    l_send(3, 3)
    l_last(0)
    s_send(0, 2)

    for c in hcs[:8]:
        c.wait_recv()
    act[0, 8 : 8 + C, :] = jnp.where(row > 0, activate(row_in[0].astype(F32)[40:80]), 0.0)
    act[21, 8 : 8 + C, :] = jnp.where(row < 7, activate(row_in[1].astype(F32)[0:40]), 0.0)
    for side, there, off in ((0, col > 0, 7), (1, col < 3, 48)):
        edge = jnp.where(there, activate(col_in[side]), 0.0)
        for r in range(R):
            act[r + 1, off : off + 1, :] = edge[r : r + 1]
    for i, (there, pick, r, spot) in enumerate((
        ((row > 0) & (col > 0), 3, 0, 7),
        ((row > 0) & (col < 3), 3, 0, 48),
        ((row < 7) & (col > 0), 0, 21, 7),
        ((row < 7) & (col < 3), 0, 21, 48),
    )):
        corner = jnp.where(there, activate(cor_in[i]), 0.0)
        act[r, spot : spot + 1, :] = corner[pick : pick + 1]

    f_done(3)
    l_send(3, 2)
    s_send(3, 0)

    def fill(p, _):
            r = jnp.where(p < 11, 2 * p, 2 * p - 21)
            for dx in range(3):
                a = act[r, 7 + dx : 7 + dx + C, :]
                b = act[r + 1, 7 + dx : 7 + dx + C, :]
                v = jnp.concatenate([a, b], axis=0).astype(BF)
                taps[dx, pl.ds(pl.multiple_of(80 * p, 80), 80), :] = v
            return 0

    lax.fori_loop(0, 21, fill, 0)

    low_half = lax.broadcasted_iota(jnp.int32, (16, 128), 0) < 8

    def delta(k):
        return jnp.where(k == 0, 0, jnp.where(k == 1, 3, jnp.where(k == 2, 1, 2)))

    def merge(k, _):
        z = lax.rem(zh + delta(k), 4)

        for m in range(2):
            base = pl.multiple_of(jnp.where(k == 0, 0, 128 + 160 * k) + 80 * m, 16)
            rows = pl.ds(base, 80)
            ya, yb = 2 * m, 2 * m + 1

            def two(j, _):
                for n in range(5):
                    if n < 3:
                        a = wall.at[0, z, j, ya, pl.ds(80 * n, 80)]
                        b = wall.at[0, z, j, yb, pl.ds(80 * n, 80)]
                    else:
                        a = wall.at[1, z, ya, j, pl.ds(80 * (n - 3), 80)]
                        b = wall.at[1, z, yb, j, pl.ds(80 * (n - 3), 80)]
                    a2, b2 = a[32:48, :].astype(F32), b[32:48, :].astype(F32)
                    mid_s = jnp.where(low_half, a2, b2).astype(BF)
                    mid_t = jnp.concatenate([a2[8:16], b2[0:8]], axis=0).astype(BF)
                    ln = pl.ds(128 * n, 128)
                    wm[2 * j, rows, ln] = jnp.concatenate(
                        [a[0:32, :], mid_s, b[0:32, :]], axis=0
                    )
                    wm[2 * j + 1, rows, ln] = jnp.concatenate(
                        [a[48:80, :], mid_t, b[48:80, :]], axis=0
                    )
                return 0

            lax.fori_loop(0, 4, two, 0)

            def tile(y_, n, r):
                i = 3 * n + r
                return wall[1, z, y_, i // 4, pl.ds(160 + 16 * (i % 4), 16), :]

            for n in range(5):
                mid = jnp.where(low_half, tile(ya, n, 2).astype(F32), tile(yb, n, 0).astype(F32))
                wm[8, rows, pl.ds(128 * n, 128)] = jnp.concatenate(
                    [tile(ya, n, 0), tile(ya, n, 1), mid.astype(BF), tile(yb, n, 1), tile(yb, n, 2)],
                    axis=0,
                )
        return 0

    def conv(w, dy):
        lane_at = jnp.where(w == 0, 0, jnp.where(w == 1, 128, 384))
        win = pl.ds(pl.multiple_of(lane_at, 128), 256)
        start = pl.multiple_of(jnp.where(dy == 0, 0, jnp.where(dy == 1, 880, 80)), 80)
        parts = [taps[dx, pl.ds(start, R * C), win] for dx in range(3)]
        rhs = wm[pl.ds(3 * dy, 3), pl.ds(pl.multiple_of(256 * w, 256), 256), :].reshape(768, CH)
        acc[...] += dot(jnp.concatenate(parts, axis=1), rhs)

    def arrive(k):
        l_fwd(k, 0, 1, 3, 2)
        l_other(k)
        s_send(k, 1, 3)
        l_last(k)
        s_send(k, 2)

    def step(t, _):
        w, dy = t // 3, lax.rem(t, 3)

        def when(there, *fs):
            @pl.when(t == there)
            def _():
                for f in fs:
                    f()

        when(0, lambda: s_wait(0))
        when(2, lambda: arrive(1))
        when(3, lambda: arrive(2), lambda: s_wait(1), lambda: s_wait(2))
        when(4, lambda: arrive(3))
        when(6, lambda: s_wait(3))

        @pl.when(dy == 0)
        def _():
            lo = jnp.where(w == 0, 0, jnp.where(w == 1, 1, 3))
            hi = jnp.where(w == 0, 1, jnp.where(w == 1, 3, 4))
            lax.fori_loop(lo, hi, merge, 0)

        conv(w, dy)
        return 0

    lax.fori_loop(0, 9, step, 0)

    def finish(r, _):
        out4[0, r] = acc[pl.ds(pl.multiple_of(C * r, 8), C), :].astype(BF)
        return 0

    lax.fori_loop(0, R, finish, 0)

    for blk in (wall.at[0], wall.at[1, pl.ds(0, 3)], wall.at[1, 3, pl.ds(0, 3)]):
        copy(blk, blk, w_s, z_r.at[0], sib).wait_send()
    for c in hcs:
        c.wait_send()
    copy(st_in.at[pl.ds(1, 31)], st_in.at[pl.ds(1, 31)], t_s, t_r, sib).wait_send()


def local(features, hole_mask, norm_gain, norm_shift, conv_weight, mask_weight, conv_bias):
    vm = pl.BlockSpec(memory_space=pltpu.VMEM)
    dma = pltpu.SemaphoreType.DMA
    result = pl.pallas_call(
        kernel,
        out_shape=jax.ShapeDtypeStruct((1, R, C, CH), BF),
        in_specs=[pl.BlockSpec(memory_space=pl.ANY)] + [vm] * 6,
        out_specs=vm,
        scratch_shapes=[
            pltpu.VMEM((2, 4, 4, 4, BLK, 128), BF),
            pltpu.VMEM((9, 768, CH), BF),
            pltpu.VMEM((22, STRIDE, CH), F32),
            pltpu.VMEM((3, 42 * C, CH), BF),
            pltpu.VMEM((R * C, CH), F32),
            pltpu.VMEM((R, C), jnp.int32),
            pltpu.VMEM((R // 2, 2 * C, CH), BF),
            pltpu.VMEM((2, 24, CH), F32),
            pltpu.VMEM((2, 2 * C, CH), BF),
            pltpu.VMEM((2, 24, CH), F32),
            pltpu.VMEM((4, 8, CH), F32),
            pltpu.VMEM((8, R, C), jnp.int32),
            pltpu.VMEM((128, 128), F32),
            pltpu.VMEM((128, 128), F32),
            pltpu.VMEM((R * C, 128), BF),
            pltpu.VMEM((128, CH), F32),
            pltpu.VMEM((8, 128), F32),
            pltpu.VMEM((32, 8, 128), F32),
            dma(()), dma((3,)), dma((4, 2)), dma((4, 2)), dma((4, 4, 2)), dma((4, 4)), dma((4,)),
            dma((16,)), dma((8,)), dma(()), dma(()), dma(()), dma(()),
            pltpu.VMEM((R, C, CH), BF),
        ],
        compiler_params=pltpu.CompilerParams(
            collective_id=0, has_side_effects=True, vmem_limit_bytes=56 << 20
        ),
        name="conv",
    )(features, hole_mask.reshape(R, 1, C), norm_gain, norm_shift, conv_weight, mask_weight, conv_bias)
    return result


def solution(mesh):
    image = P("dp", "row", "col", None)
    return jax.shard_map(
        local,
        mesh=mesh,
        in_specs=(image, P("dp", "row", "col"), P(), P(), P(None, "dp", None), P(), P()),
        out_specs=image,
        check_vma=False,
    )
```
